256 devices in a mesh: row: 32 (over z, y_lo, core), col: 8 (over y_hi, x).
Axes of the slice: x: 4, y: 4 (y_hi: 2, y_lo: 2; y = y_hi * 2 + y_lo), z: 8, core: 2. Of those that a mesh axis runs over, the one named last changes fastest.
Arguments:
- affinity_tiles: bfloat16 [1024, 64, 128, 128], P('row', 'col'), may hold values from -30 to 30
- block_columns: int32 [1024, 64], P('row', 'col'), may hold values from 0 to 1023, as said below
- slot_counts: int32 [1024, 8], P('row', 'col'), may hold values from 1 to 8
- start_vectors: float32 [1024, 64, 128], P(('row', 'col')), may hold values from -70 to 70
Outputs:
- embedding: float32 [1024, 64, 128], P(('row', 'col'))
- upper_factor: float32 [64, 64], replicated
The draws below stay inside these ranges and needn't reach their ends.
Inputs may be any that keep to these rules, and one draw needn't show every extreme that they name: `block_columns`: the slots of group g of a block row (slots g * 8 to g * 8 + 7) name blocks j with (j // 4) % 8 == g.
All inputs are finite; a program needn't handle non-finite values.
Results may differ from the reference program's by a relative error of at most 0.004.
Values may be sent and summed in bfloat16 or wider, within the bound.
A program may use at most 64 MiB of HBM per device.

```python
import math
import jax
import jax.numpy as jnp
from jax import lax

BS = 128
VECS = 64
NEIGH = 64
BR_DEV = 32
ITERS = 2
GROUPS = 8
SLOTS = 8
BP = 4
NB = 1024


def draw_affinity_tiles(key, part):
    key = jax.random.fold_in(key, 11)
    first, second = jax.random.split(key, 2)
    shape = (NB, NEIGH, BS, BS)
    level = jnp.arange(NB, dtype=jnp.float32) / max(NB - 1, 1)
    entries = jax.random.truncated_normal(first, -4.0, 4.0, shape, jnp.float32)
    rising = jnp.exp(level * math.log(3.0))
    spread = jnp.exp(jax.random.uniform(second, (NB, 1, BS, 1), jnp.float32, 0.0, math.log(10.0)))
    return (entries * spread * rising[:, None, None, None] / math.sqrt(BS * SLOTS)).astype(jnp.bfloat16)


def draw_block_columns(key, part):
    key = jax.random.fold_in(key, 23)
    first, second = jax.random.split(key, 2)
    owners = jax.random.randint(first, (NB, NEIGH), 0, NB // BR_DEV)
    within = jax.random.randint(second, (NB, NEIGH), 0, BP)
    group_index = jnp.arange(NEIGH, dtype=jnp.int32) // SLOTS
    return ((owners * GROUPS + group_index[None, :]) * BP + within).astype(jnp.int32)


def draw_start_vectors(key, part):
    key = jax.random.fold_in(key, 37)
    first, second = jax.random.split(key, 2)
    shape = (NB, VECS, BS)
    column_scale = jnp.exp(jax.random.uniform(second, (1, VECS, 1), jnp.float32, 0.0, math.log(10.0)))
    entries = jax.random.truncated_normal(first, -4.0, 4.0, shape, jnp.float32)
    return entries * column_scale


def plant(drawn, own_key, smallest, high):
    dims = drawn.shape
    index_at = [jax.random.randint(jax.random.fold_in(own_key, axis), (), 0, dims[axis]) for axis in range(len(dims))]
    drawn = drawn.at[tuple(index_at)].set(smallest)
    longest = dims.index(max(dims))
    index_at[longest] = (index_at[longest] + 1) % dims[longest]
    return drawn.at[tuple(index_at)].set(high)


def setup_inputs(seed: int = 0) -> dict:
    seeds = jax.random.split(jax.random.key(seed), 5)
    affinity_tiles = draw_affinity_tiles(jax.random.fold_in(seeds[4], 71), 0)
    block_columns = draw_block_columns(jax.random.fold_in(seeds[4], 71), 0)
    slot_counts = plant(jax.random.randint(seeds[2], (NB, GROUPS), 1, SLOTS + 1), jax.random.fold_in(seeds[2], 1), 1, SLOTS).astype(jnp.int32)
    start_vectors = draw_start_vectors(jax.random.fold_in(seeds[4], 71), 0)
    return dict(affinity_tiles=affinity_tiles, block_columns=block_columns, slot_counts=slot_counts, start_vectors=start_vectors)


def block_products(affinity_tiles, block_columns, slot_counts, vectors):
    rounded = vectors.astype(jnp.bfloat16)
    positions = jnp.arange(NEIGH)
    group_index = positions // SLOTS
    within = positions % SLOTS
    occupied = within[None, :] < jnp.take(slot_counts, group_index, axis=1)
    outer = NB // BR_DEV
    tiles_grouped = affinity_tiles.reshape(outer, BR_DEV, NEIGH, BS, BS)
    columns_grouped = block_columns.reshape(outer, BR_DEV, NEIGH)
    occupied_grouped = occupied.reshape(outer, BR_DEV, NEIGH)

    def one_group(pieces):
        tile_part, column_part, occupied_part = pieces
        fetched = jnp.take(rounded, column_part.astype(jnp.int32), axis=0)
        fetched = jnp.where(occupied_part[:, :, None, None], fetched, jnp.zeros_like(fetched))
        return jnp.einsum('bsik,bsvk->bvi', tile_part.astype(jnp.float32), fetched.astype(jnp.float32))
    result = lax.map(one_group, (tiles_grouped, columns_grouped, occupied_grouped))
    return result.reshape(NB, VECS, BS)

def orthonormalize(image):
    gram = jnp.einsum('bvi,bwi->vw', image, image, precision=lax.Precision.HIGHEST)
    lower_factor = jnp.linalg.cholesky(gram)
    inverse_lower = jax.scipy.linalg.solve_triangular(lower_factor, jnp.eye(VECS, dtype=jnp.float32), lower=True)
    orthonormal = jnp.einsum('bwi,vw->bvi', image, inverse_lower, precision=lax.Precision.HIGHEST)
    return (orthonormal, lower_factor.T)

def reference(affinity_tiles, block_columns, slot_counts, start_vectors):
    vectors = start_vectors
    upper = jnp.eye(VECS, dtype=jnp.float32)
    for iteration in range(ITERS):
        image = block_products(affinity_tiles, block_columns, slot_counts, vectors)
        vectors, upper = orthonormalize(image)
    scaling = math.sqrt(NB * BS)
    return (vectors * scaling, upper / scaling)
```

```python
import functools
import math

import jax
import jax.numpy as jnp
from jax import lax
from jax.experimental import pallas as pl
from jax.experimental.pallas import tpu as pltpu
from jax.sharding import PartitionSpec as P

ITERS = 2
MESH = pl.DeviceIdType.MESH
F32 = jnp.float32
BF16 = jnp.bfloat16
HIGHEST = lax.Precision.HIGHEST
X, Y, Z = 4, 4, 8
COLS = 8
SLOTS = 8
BP = 4
ROWS = 32

GATHER = (
    ((0, 0), (("z", 1), ("z", -1), ("y", 0), ("z", 2), ("z", -2), ("s", 0))),
    ((0, 7), (("y", 0), ("s", 0))),
    ((0, 1), (("y", 0), ("s", 0))),
    ((1, 0), (("s", 0),)),
    ((0, 6), (("z", 1), ("z", 2), ("y", 0), ("s", 0))),
    ((0, 2), (("z", -1), ("y", 0), ("s", 0))),
    ((1, 7), (("s", 0),)),
    ((1, 1), (("s", 0),)),
    ((0, 5), (("y", 0), ("s", 0))),
    ((0, 3), (("y", 0), ("s", 0))),
    ((1, 2), (("s", 0),)),
    ((1, 6), (("s", 0),)),
    ((0, 4), (("y", 0), ("s", 0))),
    ((1, 3), (("s", 0),)),
    ((1, 5), (("s", 0),)),
    ((1, 4), (("s", 0),)),
)
GATHER_SENDS = sum(len(targets) for _, targets in GATHER)


def coords():
    row, col = lax.axis_index("row"), lax.axis_index("col")
    return lax.rem(col, 4), col // 4 * 2 + lax.rem(row // 2, 2), row // 4, lax.rem(row, 2)


def device(x, y, z, core):
    return (z * 4 + lax.rem(y, 2) * 2 + core, y // 2 * 4 + x)


def remote(src, dst, send_sem, recv_sem, to):
    return pltpu.make_async_remote_copy(
        src_ref=src, dst_ref=dst, send_sem=send_sem, recv_sem=recv_sem, device_id=to, device_id_type=MESH
    )


def gather(blocks, send_sem, recv_sem):
    x, y, z, core = coords()
    partner = y // 2 * 2 + 1 - lax.rem(y, 2)

    def place(piece, core):
        column, dz = piece
        y_of = y if column == 0 else partner
        row = lax.rem(z + dz, Z) * 4 + lax.rem(y_of, 2) * 2 + core
        return blocks.at[pl.ds(row * BP, BP)]

    def wait(piece, of_core, index):
        here = place(piece, of_core)
        remote(here, here, send_sem.at[0], recv_sem.at[index], device(x, y, z, 1 - core)).wait_recv()

    copies = []
    for piece, targets in GATHER:
        column, dz = piece
        if piece != (0, 0):
            wait(piece, core, column * Z + dz)
        here = place(piece, core)
        for kind, step in targets:
            if kind == "z":
                to, index = device(x, y, lax.rem(z + step + Z, Z), core), column * Z + (dz - step) % Z
            elif kind == "y":
                to, index = device(x, partner, z, core), (1 - column) * Z + dz
            else:
                to, index = device(x, y, z, 1 - core), 2 * Z + column * Z + dz
            copy = remote(here, here, send_sem.at[len(copies)], recv_sem.at[index], to)
            copy.start()
            copies.append(copy)
    for piece, _ in GATHER:
        wait(piece, 1 - core, 2 * Z + piece[0] * Z + piece[1])
    for copy in copies:
        copy.wait_send()


def partial_images(index, tiles, blocks, partial, arrived, send_sem, recv_sem):
    x, y, z, core = coords()
    col = lax.axis_index("col")

    def peer(offset):
        to_x, to_hi = lax.rem(x + offset, X), lax.rem(y // 2 + offset // X, 2)
        return to_hi * X + to_x, device(to_x, to_hi * 2 + lax.rem(y, 2), z, core)

    def copy(offset):
        owner, to = peer(offset)
        return remote(
            partial.at[pl.ds(owner * BP, BP)], arrived.at[offset], send_sem.at[offset], recv_sem.at[offset], to
        )

    def products(owner):
        for within in range(BP):
            b = owner * BP + within
            vectors = jnp.concatenate([blocks[index[b, s]] for s in range(SLOTS)], axis=1)
            tile_row = jnp.concatenate([tiles[b, s] for s in range(SLOTS)], axis=1)
            image = lax.dot_general(vectors, tile_row, (((1,), (1,)), ((), ())), preferred_element_type=F32)
            partial[b] = image

    def step(i, carry):
        offset = COLS - 1 - i
        products(peer(offset)[0])
        copy(offset).start()
        return carry

    lax.fori_loop(0, COLS - 1, step, 0)
    products(col)
    total = partial[pl.ds(col * BP, BP)]
    for offset in range(COLS - 1, 0, -1):
        copy(offset).wait_recv()
        total = total + arrived[offset]
    for offset in range(1, COLS):
        copy(offset).wait_send()
    return total


def sum_everywhere(gram, mine, other, plane, line, send_sem, recv_sem):
    x, y, z, core = coords()
    half = gram.shape[0] // 2
    mine[...] = jnp.concatenate([gram[:half], gram[half:]], axis=1)
    swap = remote(mine, other, send_sem.at[0], recv_sem.at[0], device(x, y, z, 1 - core))
    swap.start()
    swap.wait()
    here = y * X + x
    plane[here] = mine[...] + other[...]

    def plane_copy(offset):
        to_x, to_y = lax.rem(x + offset, X), lax.rem(y + offset // X, Y)
        return remote(plane.at[here], plane.at[here], send_sem.at[offset], recv_sem.at[1 + here], device(to_x, to_y, z, core))

    def plane_from(offset):
        source = lax.rem(y + offset // X, Y) * X + lax.rem(x + offset, X)
        return remote(plane.at[source], plane.at[source], send_sem.at[offset], recv_sem.at[1 + source], device(x, y, z, 1 - core))

    for offset in range(1, X * Y):
        plane_copy(offset).start()
    for offset in range(1, X * Y):
        plane_from(offset).wait_recv()
    for offset in range(1, X * Y):
        plane_copy(offset).wait_send()
    total = plane[0]
    for i in range(1, X * Y):
        total = total + plane[i]
    line[z] = total

    def line_copy(offset):
        return remote(
            line.at[z], line.at[z], send_sem.at[offset], recv_sem.at[1 + X * Y + z], device(x, y, lax.rem(z + offset, Z), core)
        )

    def line_from(offset):
        source = lax.rem(z + offset, Z)
        return remote(
            line.at[source], line.at[source], send_sem.at[offset], recv_sem.at[1 + X * Y + source], device(x, y, z, 1 - core)
        )

    for offset in range(1, Z):
        line_copy(offset).start()
    for offset in range(1, Z):
        line_from(offset).wait_recv()
    for offset in range(1, Z):
        line_copy(offset).wait_send()
    total = line[0]
    for i in range(1, Z):
        total = total + line[i]
    vecs = gram.shape[1]
    return jnp.concatenate([total[:, :vecs], total[:, vecs:]], axis=0)


def factor(gram):
    n = gram.shape[0]
    shape = (n, 2 * n)
    rows, cols = lax.broadcasted_iota(jnp.int32, shape, 0), lax.broadcasted_iota(jnp.int32, shape, 1)
    work = jnp.concatenate([gram, jnp.where(cols == rows, 1.0, 0.0).astype(F32)[:, :n]], axis=1)
    for j in range(0, n, 2):
        low = (j + 1) // 8 * 8
        rest = work[low:]
        first, second = work[j : j + 1], work[j + 1 : j + 2]
        a = jnp.broadcast_to(first[:, j : j + 1], first.shape)
        b = jnp.broadcast_to(first[:, j + 1 : j + 2], first.shape)
        c = jnp.broadcast_to(second[:, j + 1 : j + 2], first.shape)
        inv_a = 1.0 / a
        ratio = b * inv_a
        second = second - ratio * first
        inv_c = 1.0 / (c - ratio * b)
        col_a = jnp.broadcast_to(rest[:, j : j + 1], rest.shape)
        col_c = jnp.broadcast_to(rest[:, j + 1 : j + 2], rest.shape) - col_a * ratio
        below = rows[low:]
        rest = (
            rest
            - jnp.where(below > j, col_a, 0.0) * (first * inv_a)
            - jnp.where(below > j + 1, col_c, 0.0) * (second * inv_c)
        )
        work = jnp.concatenate([work[:low], rest], axis=0) if low else rest
    pivots = jnp.sum(jnp.where(rows == cols, work, 0.0), axis=1, keepdims=True)
    work = work * lax.rsqrt(pivots)
    upper = jnp.where(rows <= cols, work, 0.0)[:, :n]
    return upper, work[:, n:]


def kernel(scaling, index, start, tiles_in, embedding, upper_out, tiles, blocks, partial, arrived, mine, other, plane, line,
           tile_sem, gather_send, gather_recv, image_send, image_recv, sum_send, sum_recv):
    x, y, z, core = coords()
    barrier = pltpu.get_barrier_semaphore()
    met = [device(x, y, z, 1 - core)]
    met += [device(lax.rem(x + o, X), lax.rem(y + o // X, Y), z, core) for o in range(1, X * Y)]
    met += [device(x, y, lax.rem(z + o, Z), core) for o in range(1, Z)]
    for to in met:
        pl.semaphore_signal(barrier, inc=1, device_id=to, device_id_type=MESH)
    load = pltpu.make_async_copy(tiles_in, tiles, tile_sem)
    load.start()

    row = lax.axis_index("row")
    own = pl.ds(row * BP, BP)
    blocks[0, own] = start[...].astype(BF16)
    none = jnp.zeros(blocks.shape[2:], BF16)
    for it in range(ITERS):
        blocks[it, ROWS * BP] = none
    pl.semaphore_wait(barrier, len(met))
    for it in range(ITERS):
        gather(blocks.at[it], gather_send, gather_recv.at[it])
        if it == 0:
            load.wait()
        image = partial_images(index, tiles, blocks.at[it], partial, arrived.at[it], image_send, image_recv.at[it])
        wide = jnp.concatenate([image[b] for b in range(BP)], axis=1)
        gram = lax.dot_general(wide, wide, (((1,), (1,)), ((), ())), precision=HIGHEST, preferred_element_type=F32)
        gram = sum_everywhere(
            gram, mine.at[it], other.at[it], plane.at[it], line.at[it], sum_send, sum_recv.at[it]
        )
        upper, inverse = factor(gram)
        vectors = jnp.dot(inverse, wide, precision=HIGHEST, preferred_element_type=F32)
        size = image.shape[2]
        if it < ITERS - 1:
            for b in range(BP):
                blocks[it + 1, row * BP + b] = vectors[:, b * size : (b + 1) * size].astype(BF16)
        else:
            for b in range(BP):
                embedding[b] = vectors[:, b * size : (b + 1) * size] * scaling
            upper_out[...] = upper * (1.0 / scaling)


def body(affinity_tiles, block_columns, slot_counts, start_vectors):
    rows, slots = block_columns.shape
    pieces, vecs, size = start_vectors.shape
    live = lax.broadcasted_iota(jnp.int32, block_columns.shape, 1) < slot_counts
    index = jnp.where(live, block_columns // (COLS * BP) * BP + block_columns % BP, ROWS * BP)
    scaling = math.sqrt(ROWS * COLS * BP * size)
    vmem = pl.BlockSpec(memory_space=pltpu.VMEM)
    dma = pltpu.SemaphoreType.DMA
    half = (vecs // 2, 2 * vecs)
    return pl.pallas_call(
        functools.partial(kernel, scaling),
        out_shape=(
            jax.ShapeDtypeStruct(start_vectors.shape, F32),
            jax.ShapeDtypeStruct((vecs, vecs), F32),
        ),
        in_specs=[pl.BlockSpec(memory_space=pltpu.SMEM), vmem, pl.BlockSpec(memory_space=pl.ANY)],
        out_specs=(vmem, vmem),
        scratch_shapes=[
            pltpu.VMEM(affinity_tiles.shape, BF16),
            pltpu.VMEM((ITERS, ROWS * BP + 1, vecs, size), BF16),
            pltpu.VMEM((rows, vecs, size), F32),
            pltpu.VMEM((ITERS, COLS, pieces, vecs, size), F32),
            pltpu.VMEM((ITERS,) + half, F32),
            pltpu.VMEM((ITERS,) + half, F32),
            pltpu.VMEM((ITERS, X * Y) + half, F32),
            pltpu.VMEM((ITERS, Z) + half, F32),
            dma,
            dma((GATHER_SENDS,)),
            dma((ITERS, 4 * Z)),
            dma((COLS,)),
            dma((ITERS, COLS)),
            dma((X * Y,)),
            dma((ITERS, 1 + X * Y + Z)),
        ],
        compiler_params=pltpu.CompilerParams(
            collective_id=0, has_side_effects=True, vmem_limit_bytes=48 * 1024 * 1024
        ),
        name="subspace",
    )(index, start_vectors, affinity_tiles)


def solution(mesh):
    in_specs = (
        P("row", "col", None, None),
        P("row", "col"),
        P("row", "col"),
        P(("row", "col"), None, None),
    )
    out_specs = (P(("row", "col"), None, None), P())
    return jax.shard_map(body, mesh=mesh, in_specs=in_specs, out_specs=out_specs, check_vma=False)
```

```python
import functools
import math

import jax
import jax.numpy as jnp
from jax import lax
from jax.experimental import pallas as pl
from jax.experimental.pallas import tpu as pltpu
from jax.sharding import PartitionSpec as P

ITERS = 2
MESH = pl.DeviceIdType.MESH
F32 = jnp.float32
BF16 = jnp.bfloat16
HIGHEST = lax.Precision.HIGHEST
X, Y, Z = 4, 4, 8
COLS = 8
SLOTS = 8
BP = 4
ROWS = 32
MAX_GROWTH = 1.3
NARROW = False

GATHER = (
    ((0, 0), (("z", 1), ("z", -1), ("y", 0), ("z", 2), ("z", -2), ("s", 0))),
    ((0, 7), (("y", 0), ("s", 0))),
    ((0, 1), (("y", 0), ("s", 0))),
    ((1, 0), (("s", 0),)),
    ((0, 6), (("z", 1), ("z", 2), ("y", 0), ("s", 0))),
    ((0, 2), (("z", -1), ("y", 0), ("s", 0))),
    ((1, 7), (("s", 0),)),
    ((1, 1), (("s", 0),)),
    ((0, 5), (("y", 0), ("s", 0))),
    ((0, 3), (("y", 0), ("s", 0))),
    ((1, 2), (("s", 0),)),
    ((1, 6), (("s", 0),)),
    ((0, 4), (("y", 0), ("s", 0))),
    ((1, 3), (("s", 0),)),
    ((1, 5), (("s", 0),)),
    ((1, 4), (("s", 0),)),
)
GATHER_SENDS = sum(len(targets) for _, targets in GATHER)


def coords():
    row, col = lax.axis_index("row"), lax.axis_index("col")
    return lax.rem(col, 4), col // 4 * 2 + lax.rem(row // 2, 2), row // 4, lax.rem(row, 2)


def device(x, y, z, core):
    return (z * 4 + lax.rem(y, 2) * 2 + core, y // 2 * 4 + x)


def remote(src, dst, send_sem, recv_sem, to):
    return pltpu.make_async_remote_copy(
        src_ref=src, dst_ref=dst, send_sem=send_sem, recv_sem=recv_sem, device_id=to, device_id_type=MESH
    )


def gather(blocks, send_sem, recv_sem):
    x, y, z, core = coords()
    partner = y // 2 * 2 + 1 - lax.rem(y, 2)

    def place(piece, core):
        column, dz = piece
        y_of = y if column == 0 else partner
        row = lax.rem(z + dz, Z) * 4 + lax.rem(y_of, 2) * 2 + core
        return blocks.at[pl.ds(row * BP, BP)]

    def wait(piece, of_core, index):
        here = place(piece, of_core)
        remote(here, here, send_sem.at[0], recv_sem.at[index], device(x, y, z, 1 - core)).wait_recv()

    copies = []
    for position, (piece, targets) in enumerate(GATHER):
        column, dz = piece
        if piece != (0, 0):
            wait(piece, core, column * Z + dz)
        here = place(piece, core)
        for kind, step in targets:
            if kind == "z":
                to, index = device(x, y, lax.rem(z + step + Z, Z), core), column * Z + (dz - step) % Z
            elif kind == "y":
                to, index = device(x, partner, z, core), (1 - column) * Z + dz
            else:
                to, index = device(x, y, z, 1 - core), 2 * Z + column * Z + dz
            copy = remote(here, here, send_sem.at[len(copies)], recv_sem.at[index], to)
            copy.start()
            copies.append(copy)
        yield position
    for piece, _ in GATHER:
        wait(piece, 1 - core, 2 * Z + piece[0] * Z + piece[1])
    for copy in copies:
        copy.wait_send()


def product(columns, counts, tiles, blocks, b):
    picked = []
    for s in range(SLOTS):
        name = columns[s, b]
        place = name // (COLS * BP) * BP + name % BP
        picked.append(blocks[jnp.where(s < counts[0, b], place, ROWS * BP)])
    vectors = jnp.concatenate(picked, axis=1)
    tile_row = jnp.concatenate([tiles[b, s] for s in range(SLOTS)], axis=1)
    return lax.dot_general(vectors, tile_row, (((1,), (1,)), ((), ())), preferred_element_type=F32)


def images(columns, counts, tiles, blocks, partial, arrived, send_sem, recv_sem):
    x, y, z, core = coords()
    col = lax.axis_index("col")

    def peer(offset):
        to_x, to_hi = lax.rem(x + offset, X), lax.rem(y // 2 + offset // X, 2)
        return to_hi * X + to_x, device(to_x, to_hi * 2 + lax.rem(y, 2), z, core)

    def copy(offset):
        owner, to = peer(offset)
        return remote(
            partial.at[pl.ds(owner * BP, BP)], arrived.at[offset], send_sem.at[offset], recv_sem.at[offset], to
        )

    def step(i, carry):
        offset = COLS - 1 - i
        owner = peer(offset)[0]
        for within in range(BP):
            b = owner * BP + within
            partial[b] = product(columns, counts, tiles, blocks, b).astype(partial.dtype)
        copy(offset).start()
        return carry

    lax.fori_loop(0, COLS - 1, step, 0)
    own = [product(columns, counts, tiles, blocks, col * BP + within) for within in range(BP)]
    yield
    for offset in range(COLS - 1, 0, -1):
        copy(offset).wait_recv()
        for within in range(BP):
            own[within] = own[within] + arrived[offset, within].astype(F32)
    for offset in range(1, COLS):
        copy(offset).wait_send()
    yield jnp.concatenate(own, axis=1)


def sum_everywhere(gram, mine, other, plane, line, send_sem, recv_sem):
    x, y, z, core = coords()
    half = gram.shape[0] // 2
    mine[...] = jnp.concatenate([gram[:half], gram[half:]], axis=1)
    swap = remote(mine, other, send_sem.at[0], recv_sem.at[0], device(x, y, z, 1 - core))
    swap.start()
    yield
    swap.wait()
    here = y * X + x
    plane[here] = mine[...] + other[...]

    def plane_copy(offset):
        to_x, to_y = lax.rem(x + offset, X), lax.rem(y + offset // X, Y)
        return remote(plane.at[here], plane.at[here], send_sem.at[offset], recv_sem.at[1 + here], device(to_x, to_y, z, core))

    def plane_from(offset):
        source = lax.rem(y + offset // X, Y) * X + lax.rem(x + offset, X)
        return remote(plane.at[source], plane.at[source], send_sem.at[offset], recv_sem.at[1 + source], device(x, y, z, 1 - core))

    for offset in range(1, X * Y):
        plane_copy(offset).start()
    yield
    for offset in range(1, X * Y):
        plane_from(offset).wait_recv()
    for offset in range(1, X * Y):
        plane_copy(offset).wait_send()
    total = plane[0]
    for i in range(1, X * Y):
        total = total + plane[i]
    line[z] = total

    def line_copy(offset):
        return remote(
            line.at[z], line.at[z], send_sem.at[X * Y - 1 + offset], recv_sem.at[1 + X * Y + z], device(x, y, lax.rem(z + offset, Z), core)
        )

    def line_from(offset):
        source = lax.rem(z + offset, Z)
        return remote(
            line.at[source], line.at[source], send_sem.at[offset], recv_sem.at[1 + X * Y + source], device(x, y, z, 1 - core)
        )

    for offset in range(1, Z):
        line_copy(offset).start()
    yield
    for offset in range(1, Z):
        line_from(offset).wait_recv()
    for offset in range(1, Z):
        line_copy(offset).wait_send()
    total = line[0]
    for i in range(1, Z):
        total = total + line[i]
    vecs = gram.shape[1]
    yield jnp.concatenate([total[:, :vecs], total[:, vecs:]], axis=0)


def factor(gram):
    n = gram.shape[0]
    shape = (n, 2 * n)
    rows, cols = lax.broadcasted_iota(jnp.int32, shape, 0), lax.broadcasted_iota(jnp.int32, shape, 1)
    work = jnp.concatenate([gram, jnp.where(cols == rows, 1.0, 0.0).astype(F32)[:, :n]], axis=1)
    for j in range(0, n, 2):
        low = (j + 1) // 8 * 8
        rest = work[low:]
        first, second = work[j : j + 1], work[j + 1 : j + 2]
        a = jnp.broadcast_to(first[:, j : j + 1], first.shape)
        b = jnp.broadcast_to(first[:, j + 1 : j + 2], first.shape)
        c = jnp.broadcast_to(second[:, j + 1 : j + 2], first.shape)
        inv_a = 1.0 / a
        ratio = b * inv_a
        second = second - ratio * first
        inv_c = 1.0 / (c - ratio * b)
        col_a = jnp.broadcast_to(rest[:, j : j + 1], rest.shape)
        col_c = jnp.broadcast_to(rest[:, j + 1 : j + 2], rest.shape) - col_a * ratio
        below = rows[low:]
        rest = (
            rest
            - jnp.where(below > j, col_a, 0.0) * (first * inv_a)
            - jnp.where(below > j + 1, col_c, 0.0) * (second * inv_c)
        )
        work = jnp.concatenate([work[:low], rest], axis=0) if low else rest
    pivots = jnp.sum(jnp.where(rows == cols, work, 0.0), axis=1, keepdims=True)
    work = work * lax.rsqrt(pivots)
    upper = jnp.where(rows <= cols, work, 0.0)[:, :n]
    return upper, work[:, n:]


def last(steps):
    *_, result = steps
    return result


def gram_of(image):
    return lax.dot_general(image, image, (((1,), (1,)), ((), ())), precision=HIGHEST, preferred_element_type=F32)


def kernel(deferred, scaling, columns, counts, start_in, tiles_in, embedding, upper_out, *rest):
    flag, rest = (rest[0], rest[1:]) if deferred else (None, rest)
    (start, tiles, blocks_1, blocks_2, partial, arrived, partial_2, arrived_2, mine, other, plane, line,
     load_sem, gather_send, gather_recv, image_send, image_recv, sum_send, sum_recv) = rest
    x, y, z, core = coords()
    barrier = pltpu.get_barrier_semaphore()
    met = [device(x, y, z, 1 - core)]
    met += [device(lax.rem(x + o, X), lax.rem(y + o // X, Y), z, core) for o in range(1, X * Y)]
    met += [device(x, y, lax.rem(z + o, Z), core) for o in range(1, Z)]
    load_start = pltpu.make_async_copy(start_in, start, load_sem.at[0])
    load_start.start()
    for to in met:
        pl.semaphore_signal(barrier, inc=1, device_id=to, device_id_type=MESH)
    load = pltpu.make_async_copy(tiles_in, tiles, load_sem.at[1])
    load.start()

    vecs, size = start.shape[1:]
    row = lax.axis_index("row")
    blocks = (blocks_1, blocks_2)
    none = jnp.zeros((vecs, size), BF16)
    for it in range(ITERS):
        blocks[it][ROWS * BP] = none
    load_start.wait()
    blocks_1[pl.ds(row * BP, BP)] = start[...].astype(BF16)
    pl.semaphore_wait(barrier, len(met))

    def all_sum(it, gram):
        return sum_everywhere(
            gram, mine.at[it], other.at[it], plane.at[it], line.at[it], sum_send.at[it], sum_recv.at[it]
        )

    def gathered(it):
        return gather(blocks[it], gather_send, gather_recv.at[it])

    def images_of(it):
        parts = (partial, arrived) if it == 0 else (partial_2, arrived_2)
        return images(columns, counts, tiles, blocks[it], *parts, image_send, image_recv.at[it])

    def keep(it, image):
        for b in range(BP):
            blocks[it][row * BP + b] = image[:, b * size : (b + 1) * size].astype(BF16)

    for _ in gathered(0):
        pass
    load.wait()
    image = last(images_of(0))

    if deferred:
        keep(1, image)
        pieces = gathered(1)
        next(pieces)
        first_gram = gram_of(image)
        total = all_sum(0, first_gram)
        next(total)
        for _ in range(3):
            next(pieces)
        next(total)
        for _ in pieces:
            pass
        next(total)
        shares = images_of(1)
        next(shares)
        first_gram = next(total)
        _, first_inverse = factor(first_gram)
        image = next(shares)
        gram = last(all_sum(1, gram_of(image)))
    else:
        _, inverse = factor(last(all_sum(0, gram_of(image))))
        keep(1, jnp.dot(inverse, image, precision=HIGHEST, preferred_element_type=F32))
        for _ in gathered(1):
            pass
        image = last(images_of(1))
        gram = last(all_sum(1, gram_of(image)))

    upper, inverse = factor(gram)
    vectors = jnp.dot(inverse, image, precision=HIGHEST, preferred_element_type=F32)
    for b in range(BP):
        embedding[b] = vectors[:, b * size : (b + 1) * size] * scaling
    if deferred:
        upper = lax.dot_general(
            upper, first_inverse, (((1,), (1,)), ((), ())), precision=HIGHEST, preferred_element_type=F32
        )
        diagonal = lax.broadcasted_iota(jnp.int32, gram.shape, 0) == lax.broadcasted_iota(jnp.int32, gram.shape, 1)
        lengths = jnp.sum(jnp.where(diagonal, first_gram, 0.0), axis=0, keepdims=True)
        growth = jnp.sum(first_inverse * (first_inverse * lengths)) / vecs
        entries = jnp.where(diagonal, gram, 1.0)
        safe = (growth < MAX_GROWTH) & (jnp.min(entries) > 1e-18) & (jnp.max(entries) < 1e34)
        flag[0, 0] = safe.astype(jnp.int32)
    upper_out[...] = upper * (1.0 / scaling)


def call(deferred, affinity_tiles, columns, counts, start_vectors):
    rows = affinity_tiles.shape[0]
    pieces, vecs, size = start_vectors.shape
    scaling = math.sqrt(ROWS * COLS * BP * size)
    vmem, smem = pl.BlockSpec(memory_space=pltpu.VMEM), pl.BlockSpec(memory_space=pltpu.SMEM)
    hbm = pl.BlockSpec(memory_space=pl.ANY)
    dma = pltpu.SemaphoreType.DMA
    half = (vecs // 2, 2 * vecs)
    second = BF16 if deferred and NARROW else F32
    outs = [jax.ShapeDtypeStruct(start_vectors.shape, F32), jax.ShapeDtypeStruct((vecs, vecs), F32)]
    return pl.pallas_call(
        functools.partial(kernel, deferred, scaling),
        out_shape=outs + [jax.ShapeDtypeStruct((1, 1), jnp.int32)] * deferred,
        in_specs=[smem, smem, hbm, hbm],
        out_specs=[vmem, vmem] + [smem] * deferred,
        scratch_shapes=[
            pltpu.VMEM(start_vectors.shape, F32),
            pltpu.VMEM(affinity_tiles.shape, BF16),
            pltpu.VMEM((ROWS * BP + 1, vecs, size), BF16),
            pltpu.VMEM((ROWS * BP + 1, vecs, size), BF16),
            pltpu.VMEM((rows, vecs, size), F32),
            pltpu.VMEM((COLS, pieces, vecs, size), F32),
            pltpu.VMEM((rows, vecs, size), second),
            pltpu.VMEM((COLS, pieces, vecs, size), second),
            pltpu.VMEM((ITERS,) + half, F32),
            pltpu.VMEM((ITERS,) + half, F32),
            pltpu.VMEM((ITERS, X * Y) + half, F32),
            pltpu.VMEM((ITERS, Z) + half, F32),
            dma((2,)),
            dma((GATHER_SENDS,)),
            dma((ITERS, 4 * Z)),
            dma((COLS,)),
            dma((ITERS, COLS)),
            dma((ITERS, X * Y + Z)),
            dma((ITERS, 1 + X * Y + Z)),
        ],
        compiler_params=pltpu.CompilerParams(
            collective_id=int(deferred), has_side_effects=True, vmem_limit_bytes=48 * 1024 * 1024
        ),
        name="deferred" if deferred else "in_order",
    )(columns, counts, start_vectors, affinity_tiles)


def body(affinity_tiles, block_columns, slot_counts, start_vectors):
    args = (affinity_tiles, block_columns.T, slot_counts.T, start_vectors)
    embedding, upper, safe = call(True, *args)
    return lax.cond(safe[0, 0] > 0, lambda: (embedding, upper), lambda: tuple(call(False, *args)))


def solution(mesh):
    in_specs = (
        P("row", "col", None, None),
        P("row", "col"),
        P("row", "col"),
        P(("row", "col"), None, None),
    )
    out_specs = (P(("row", "col"), None, None), P())
    return jax.shard_map(body, mesh=mesh, in_specs=in_specs, out_specs=out_specs, check_vma=False)
```

```python
import functools
import math

import jax
import jax.numpy as jnp
from jax import lax
from jax.experimental import pallas as pl
from jax.experimental.pallas import tpu as pltpu
from jax.sharding import PartitionSpec as P

ITERS = 2
MESH = pl.DeviceIdType.MESH
F32 = jnp.float32
BF16 = jnp.bfloat16
HIGHEST = lax.Precision.HIGHEST
X, Y, Z = 4, 4, 8
COLS = 8
SLOTS = 8
BP = 4
ROWS = 32
MAX_GROWTH = 1.15
NARROW = (True, True)

CHUNKS = ((0, 4),)
GATHER = (
    ((0, 0), 0, "z+2 z-2 y z+1 z-1 s"),
    ((0, 6), 0, "y z+2 z+1 s"),
    ((0, 2), 0, "y z-1 s"),
    ((0, 7), 0, "y s"),
    ((0, 1), 0, "y s"),
    ((1, 0), 0, "s"),
    ((1, 6), 0, "z+1 z+2 s"),
    ((1, 2), 0, "z-1 s"),
    ((1, 7), 0, "s"),
    ((1, 1), 0, "s"),
    ((0, 5), 0, "s"),
    ((0, 3), 0, "s"),
    ((1, 5), 0, "s"),
    ((1, 3), 0, "s"),
    ((0, 4), 0, "s"),
    ((1, 4), 0, "s"),
)
GATHER_SENDS = sum(len(targets.split()) for _, _, targets in GATHER)
GATHER_SLOTS = 4 * Z


def coords():
    row, col = lax.axis_index("row"), lax.axis_index("col")
    return lax.rem(col, 4), col // 4 * 2 + lax.rem(row // 2, 2), row // 4, lax.rem(row, 2)


def device(x, y, z, core):
    return (z * 4 + lax.rem(y, 2) * 2 + core, y // 2 * 4 + x)


def remote(src, dst, send_sem, recv_sem, to):
    return pltpu.make_async_remote_copy(
        src_ref=src, dst_ref=dst, send_sem=send_sem, recv_sem=recv_sem, device_id=to, device_id_type=MESH
    )


def gather(blocks, send_sem, recv_sem):
    x, y, z, core = coords()
    partner = y // 2 * 2 + 1 - lax.rem(y, 2)
    way = 1 - 2 * core

    def place(piece, chunk, core):
        column, dz = piece
        y_of = y if column == 0 else partner
        row = lax.rem(z + way * dz + Z, Z) * 4 + lax.rem(y_of, 2) * 2 + core
        return blocks.at[pl.ds(row * BP + CHUNKS[chunk][0], CHUNKS[chunk][1])]

    def slot(column, dz, chunk, other):
        return ((chunk * 2 + other) * 2 + column) * Z + dz

    def wait(piece, chunk, other):
        column, dz = piece
        here = place(piece, chunk, 1 - core if other else core)
        index = slot(column, -dz % Z if other else dz, chunk, other)
        remote(here, here, send_sem.at[0], recv_sem.at[index], device(x, y, z, 1 - core)).wait_recv()

    copies, held = [], [((0, 0), chunk) for chunk in range(len(CHUNKS))]
    for position, (piece, chunk, targets) in enumerate(GATHER):
        column, dz = piece
        if (piece, chunk) not in held:
            wait(piece, chunk, 0)
            held.append((piece, chunk))
        here = place(piece, chunk, core)
        for target in targets.split():
            kind, step = target[0], int(target[1:] or 0)
            if kind == "z":
                to = device(x, y, lax.rem(z + way * step + Z, Z), core)
                index = slot(column, (dz - step) % Z, chunk, 0)
            elif kind == "y":
                to, index = device(x, partner, z, core), slot(1 - column, dz, chunk, 0)
            else:
                to, index = device(x, y, z, 1 - core), slot(column, dz, chunk, 1)
            copy = remote(here, here, send_sem.at[len(copies)], recv_sem.at[index], to)
            copy.start()
            copies.append(copy)
        yield position
    for piece, chunk in held:
        wait(piece, chunk, 1)
    for copy in copies:
        copy.wait_send()


def product(columns, counts, tiles, blocks, b):
    picked = []
    for s in range(SLOTS):
        name = columns[s, b]
        place = name // (COLS * BP) * BP + name % BP
        picked.append(blocks[jnp.where(s < counts[0, b], place, ROWS * BP)])
    vectors = jnp.concatenate(picked, axis=1)
    tile_row = jnp.concatenate([tiles[b, s] for s in range(SLOTS)], axis=1)
    return lax.dot_general(vectors, tile_row, (((1,), (1,)), ((), ())), preferred_element_type=F32)


def images(columns, counts, tiles, blocks, partial, arrived, send_sem, recv_sem):
    x, y, z, core = coords()
    col = lax.axis_index("col")

    def peer(offset):
        to_x, to_hi = lax.rem(x + offset, X), lax.rem(y // 2 + offset // X, 2)
        return to_hi * X + to_x, device(to_x, to_hi * 2 + lax.rem(y, 2), z, core)

    def copy(offset):
        owner, to = peer(offset)
        return remote(
            partial.at[pl.ds(owner * BP, BP)], arrived.at[offset], send_sem.at[offset], recv_sem.at[offset], to
        )

    def step(i, carry):
        offset = COLS - 1 - i
        owner = peer(offset)[0]
        for within in range(BP):
            b = owner * BP + within
            partial[b] = product(columns, counts, tiles, blocks, b).astype(partial.dtype)
        copy(offset).start()
        return carry

    lax.fori_loop(0, COLS - 1, step, 0)
    own = [product(columns, counts, tiles, blocks, col * BP + within) for within in range(BP)]
    yield
    for offset in range(COLS - 1, 0, -1):
        copy(offset).wait_recv()
        for within in range(BP):
            own[within] = own[within] + arrived[offset, within].astype(F32)
    for offset in range(1, COLS):
        copy(offset).wait_send()
    yield jnp.concatenate(own, axis=1)


def sum_everywhere(gram, mine, other, plane, line, send_sem, recv_sem):
    x, y, z, core = coords()
    half = gram.shape[0] // 2
    mine[...] = jnp.concatenate([gram[:half], gram[half:]], axis=1)
    swap = remote(mine, other, send_sem.at[0], recv_sem.at[0], device(x, y, z, 1 - core))
    swap.start()
    yield
    swap.wait()
    here = y * X + x
    plane[here] = mine[...] + other[...]

    def plane_copy(offset):
        to_x, to_y = lax.rem(x + offset, X), lax.rem(y + offset // X, Y)
        return remote(plane.at[here], plane.at[here], send_sem.at[offset], recv_sem.at[1 + here], device(to_x, to_y, z, core))

    def plane_from(offset):
        source = lax.rem(y + offset // X, Y) * X + lax.rem(x + offset, X)
        return remote(plane.at[source], plane.at[source], send_sem.at[offset], recv_sem.at[1 + source], device(x, y, z, 1 - core))

    for offset in range(1, X * Y):
        plane_copy(offset).start()
    yield
    for offset in range(1, X * Y):
        plane_from(offset).wait_recv()
    total = plane[0]
    for i in range(1, X * Y):
        total = total + plane[i]
    line[z] = total

    def line_copy(offset):
        return remote(
            line.at[z], line.at[z], send_sem.at[X * Y - 1 + offset], recv_sem.at[1 + X * Y + z], device(x, y, lax.rem(z + offset, Z), core)
        )

    def line_from(offset):
        source = lax.rem(z + offset, Z)
        return remote(
            line.at[source], line.at[source], send_sem.at[offset], recv_sem.at[1 + X * Y + source], device(x, y, z, 1 - core)
        )

    for offset in range(1, Z):
        line_copy(offset).start()
    yield
    for offset in range(1, Z):
        line_from(offset).wait_recv()
    total = line[0]
    for i in range(1, Z):
        total = total + line[i]
    for offset in range(1, X * Y):
        plane_copy(offset).wait_send()
    for offset in range(1, Z):
        line_copy(offset).wait_send()
    vecs = gram.shape[1]
    yield jnp.concatenate([total[:, :vecs], total[:, vecs:]], axis=0)


def factor(gram):
    n = gram.shape[0]
    shape = (n, 2 * n)
    rows, cols = lax.broadcasted_iota(jnp.int32, shape, 0), lax.broadcasted_iota(jnp.int32, shape, 1)
    work = jnp.concatenate([gram, jnp.where(cols == rows, 1.0, 0.0).astype(F32)[:, :n]], axis=1)
    for j in range(0, n, 2):
        low = (j + 1) // 8 * 8
        rest = work[low:]
        first, second = work[j : j + 1], work[j + 1 : j + 2]
        a = jnp.broadcast_to(first[:, j : j + 1], first.shape)
        b = jnp.broadcast_to(first[:, j + 1 : j + 2], first.shape)
        c = jnp.broadcast_to(second[:, j + 1 : j + 2], first.shape)
        inv_a = 1.0 / a
        ratio = b * inv_a
        second = second - ratio * first
        inv_c = 1.0 / (c - ratio * b)
        col_a = jnp.broadcast_to(rest[:, j : j + 1], rest.shape)
        col_c = jnp.broadcast_to(rest[:, j + 1 : j + 2], rest.shape) - col_a * ratio
        below = rows[low:]
        rest = (
            rest
            - jnp.where(below > j, col_a, 0.0) * (first * inv_a)
            - jnp.where(below > j + 1, col_c, 0.0) * (second * inv_c)
        )
        work = jnp.concatenate([work[:low], rest], axis=0) if low else rest
    pivots = jnp.sum(jnp.where(rows == cols, work, 0.0), axis=1, keepdims=True)
    work = work * lax.rsqrt(pivots)
    upper = jnp.where(rows <= cols, work, 0.0)[:, :n]
    return upper, work[:, n:]


def advance(steps, count):
    for _ in range(count):
        next(steps)


def last(steps):
    result = None
    for result in steps:
        pass
    return result


def gram_of(image):
    return lax.dot_general(image, image, (((1,), (1,)), ((), ())), precision=HIGHEST, preferred_element_type=F32)


def growth(gram, inverse):
    diagonal = lax.broadcasted_iota(jnp.int32, gram.shape, 0) == lax.broadcasted_iota(jnp.int32, gram.shape, 1)
    lengths = jnp.sum(jnp.where(diagonal, gram, 0.0), axis=0, keepdims=True)
    return jnp.sum(inverse * (inverse * lengths)) / gram.shape[0], jnp.min(lengths), jnp.max(lengths)


def kernel(deferred, scaling, columns, counts, start_in, tiles_in, embedding, upper_out, *rest):
    flag, rest = (rest[0], rest[1:]) if deferred else (None, rest)
    (blocks_1, blocks_2, partial_1, partial_2, arrived_1, arrived_2, start, tiles, mine, other, plane, line,
     load_sem, gather_send, gather_recv, image_send, image_recv, sum_send, sum_recv) = rest
    x, y, z, core = coords()
    barrier = pltpu.get_barrier_semaphore()
    met = [device(x, y, z, 1 - core)]
    met += [device(lax.rem(x + o, X), lax.rem(y + o // X, Y), z, core) for o in range(1, X * Y)]
    met += [device(x, y, lax.rem(z + o, Z), core) for o in range(1, Z)]
    load_start = pltpu.make_async_copy(start_in, start, load_sem.at[0])
    load_start.start()
    for to in met:
        pl.semaphore_signal(barrier, inc=1, device_id=to, device_id_type=MESH)
    load = pltpu.make_async_copy(tiles_in, tiles, load_sem.at[1])
    load.start()

    vecs, size = start.shape[1:]
    row = lax.axis_index("row")
    for ref in (blocks_1, blocks_2):
        ref[ROWS * BP] = jnp.zeros((vecs, size), BF16)
    load_start.wait()
    blocks_1[pl.ds(row * BP, BP)] = start[...].astype(BF16)
    pl.semaphore_wait(barrier, len(met))

    def all_sum(it, gram):
        return sum_everywhere(
            gram, mine.at[it], other.at[it], plane.at[it], line.at[it], sum_send.at[it], sum_recv.at[it]
        )

    def gathered(it):
        return gather((blocks_1, blocks_2)[it], gather_send, gather_recv.at[it])

    def images_of(it):
        refs = ((blocks_1, partial_1, arrived_1), (blocks_2, partial_2, arrived_2))[it]
        return images(columns, counts, tiles, *refs, image_send, image_recv.at[it])

    def keep(image):
        for b in range(BP):
            blocks_2[row * BP + b] = image[:, b * size : (b + 1) * size].astype(BF16)

    last(gathered(0))
    load.wait()
    image = last(images_of(0))

    if deferred:
        keep(image)
        pieces = gathered(1)
        next(pieces)
        first_total = all_sum(0, gram_of(image))
        next(first_total)
        advance(pieces, len(GATHER) - 4)
        next(first_total)
        last(pieces)
        shares = images_of(1)
        next(shares)
        next(first_total)
        image = next(shares)
        total = all_sum(1, gram_of(image))
        advance(total, 2)
        first_gram = next(first_total)
        _, first_inverse = factor(first_gram)
        gram = last(total)
    else:
        _, inverse = factor(last(all_sum(0, gram_of(image))))
        keep(jnp.dot(inverse, image, precision=HIGHEST, preferred_element_type=F32))
        last(gathered(1))
        image = last(images_of(1))
        gram = last(all_sum(1, gram_of(image)))

    upper, inverse = factor(gram)
    vectors = jnp.dot(inverse, image, precision=HIGHEST, preferred_element_type=F32)
    for b in range(BP):
        embedding[b] = vectors[:, b * size : (b + 1) * size] * scaling
    if deferred:
        upper = lax.dot_general(
            upper, first_inverse, (((1,), (1,)), ((), ())), precision=HIGHEST, preferred_element_type=F32
        )
        first_growth, _, _ = growth(first_gram, first_inverse)
        second_growth, least, most = growth(gram, inverse)
        safe = (first_growth < MAX_GROWTH) & (second_growth < MAX_GROWTH) & (least > 1e-18) & (most < 1e34)
        flag[0, 0] = safe.astype(jnp.int32)
    upper_out[...] = upper * (1.0 / scaling)


def call(deferred, affinity_tiles, columns, counts, start_vectors):
    rows = affinity_tiles.shape[0]
    pieces, vecs, size = start_vectors.shape
    scaling = math.sqrt(ROWS * COLS * BP * size)
    vmem, smem = pl.BlockSpec(memory_space=pltpu.VMEM), pl.BlockSpec(memory_space=pltpu.SMEM)
    hbm = pl.BlockSpec(memory_space=pl.ANY)
    dma = pltpu.SemaphoreType.DMA
    half = (vecs // 2, 2 * vecs)
    sent = [BF16 if deferred and narrow else F32 for narrow in NARROW]
    outs = [jax.ShapeDtypeStruct(start_vectors.shape, F32), jax.ShapeDtypeStruct((vecs, vecs), F32)]
    return pl.pallas_call(
        functools.partial(kernel, deferred, scaling),
        out_shape=outs + [jax.ShapeDtypeStruct((1, 1), jnp.int32)] * deferred,
        in_specs=[smem, smem, hbm, hbm],
        out_specs=[vmem, vmem] + [smem] * deferred,
        scratch_shapes=[pltpu.VMEM((ROWS * BP + 1, vecs, size), BF16)] * ITERS
        + [pltpu.VMEM((rows, vecs, size), dtype) for dtype in sent]
        + [pltpu.VMEM((COLS, pieces, vecs, size), dtype) for dtype in sent]
        + [
            pltpu.VMEM(start_vectors.shape, F32),
            pltpu.VMEM(affinity_tiles.shape, BF16),
            pltpu.VMEM((ITERS,) + half, F32),
            pltpu.VMEM((ITERS,) + half, F32),
            pltpu.VMEM((ITERS, X * Y) + half, F32),
            pltpu.VMEM((ITERS, Z) + half, F32),
            dma((2,)),
            dma((GATHER_SENDS,)),
            dma((ITERS, len(CHUNKS) * GATHER_SLOTS)),
            dma((COLS,)),
            dma((ITERS, COLS)),
            dma((ITERS, X * Y + Z)),
            dma((ITERS, 1 + X * Y + Z)),
        ],
        compiler_params=pltpu.CompilerParams(
            collective_id=int(deferred), has_side_effects=True, vmem_limit_bytes=48 * 1024 * 1024
        ),
        name="deferred" if deferred else "in_order",
    )(columns, counts, start_vectors, affinity_tiles)


def body(affinity_tiles, block_columns, slot_counts, start_vectors):
    args = (affinity_tiles, block_columns.T, slot_counts.T, start_vectors)
    embedding, upper, safe = call(True, *args)
    return lax.cond(safe[0, 0] > 0, lambda: (embedding, upper), lambda: tuple(call(False, *args)))


def solution(mesh):
    in_specs = (
        P("row", "col", None, None),
        P("row", "col"),
        P("row", "col"),
        P(("row", "col"), None, None),
    )
    out_specs = (P(("row", "col"), None, None), P())
    return jax.shard_map(body, mesh=mesh, in_specs=in_specs, out_specs=out_specs, check_vma=False)
```

```python
import functools
import math

import jax
import jax.numpy as jnp
from jax import lax
from jax.experimental import pallas as pl
from jax.experimental.pallas import tpu as pltpu
from jax.sharding import PartitionSpec as P

ITERS = 2
MESH = pl.DeviceIdType.MESH
F32 = jnp.float32
BF16 = jnp.bfloat16
HIGHEST = lax.Precision.HIGHEST
X, Y, Z = 4, 4, 8
COLS = 8
SLOTS = 8
BP = 4
ROWS = 32
PIVOTS = 8
MAX_GROWTH = 1.15
NARROW = (True, True)

CHUNKS = ((0, 4),)
GATHER = (
    ((0, 0), 0, (("z", 2), ("z", -2), ("y", 0), ("z", 1), ("z", -1), ("s", 0))),
    ((0, 6), 0, (("y", 0), ("z", 2), ("z", 1), ("s", 0))),
    ((0, 2), 0, (("y", 0), ("z", -1), ("s", 0))),
    ((0, 7), 0, (("y", 0), ("s", 0))),
    ((0, 1), 0, (("y", 0), ("s", 0))),
    ((1, 0), 0, (("s", 0),)),
    ((1, 6), 0, (("z", 1), ("z", 2), ("s", 0))),
    ((1, 2), 0, (("z", -1), ("s", 0))),
    ((1, 7), 0, (("s", 0),)),
    ((1, 1), 0, (("s", 0),)),
    ((0, 5), 0, (("s", 0),)),
    ((0, 3), 0, (("s", 0),)),
    ((1, 5), 0, (("s", 0),)),
    ((1, 3), 0, (("s", 0),)),
    ((0, 4), 0, (("s", 0),)),
    ((1, 4), 0, (("s", 0),)),
)
GATHER_SENDS = sum(len(targets) for _, _, targets in GATHER)
GATHER_SLOTS = 4 * Z

PLANE_ORDER = (10, 6, 9, 11, 14, 2, 5, 7, 8, 13, 15, 1, 3, 4, 12)
LINE_ORDER = (4, 3, 5, 2, 6, 1, 7)


def coords():
    row, col = lax.axis_index("row"), lax.axis_index("col")
    return lax.rem(col, 4), col // 4 * 2 + lax.rem(row // 2, 2), row // 4, lax.rem(row, 2)


def device(x, y, z, core):
    return (z * 4 + lax.rem(y, 2) * 2 + core, y // 2 * 4 + x)


def remote(src, dst, send_sem, recv_sem, to):
    return pltpu.make_async_remote_copy(
        src_ref=src, dst_ref=dst, send_sem=send_sem, recv_sem=recv_sem, device_id=to, device_id_type=MESH
    )


def gather(blocks, send_sem, recv_sem):
    x, y, z, core = coords()
    partner = y // 2 * 2 + 1 - lax.rem(y, 2)
    way = 1 - 2 * core

    def place(piece, chunk, core):
        column, dz = piece
        y_of = y if column == 0 else partner
        row = lax.rem(z + way * dz + Z, Z) * 4 + lax.rem(y_of, 2) * 2 + core
        return blocks.at[pl.ds(row * BP + CHUNKS[chunk][0], CHUNKS[chunk][1])]

    def slot(column, dz, chunk, other):
        return ((chunk * 2 + other) * 2 + column) * Z + dz

    def wait(piece, chunk, other):
        column, dz = piece
        here = place(piece, chunk, 1 - core if other else core)
        index = slot(column, -dz % Z if other else dz, chunk, other)
        remote(here, here, send_sem.at[0], recv_sem.at[index], device(x, y, z, 1 - core)).wait_recv()

    copies, held = [], [((0, 0), chunk) for chunk in range(len(CHUNKS))]
    for position, (piece, chunk, targets) in enumerate(GATHER):
        column, dz = piece
        if (piece, chunk) not in held:
            wait(piece, chunk, 0)
            held.append((piece, chunk))
        here = place(piece, chunk, core)
        for kind, step in targets:
            if kind == "z":
                to = device(x, y, lax.rem(z + way * step + Z, Z), core)
                index = slot(column, (dz - step) % Z, chunk, 0)
            elif kind == "y":
                to, index = device(x, partner, z, core), slot(1 - column, dz, chunk, 0)
            else:
                to, index = device(x, y, z, 1 - core), slot(column, dz, chunk, 1)
            copy = remote(here, here, send_sem.at[len(copies)], recv_sem.at[index], to)
            copy.start()
            copies.append(copy)
        yield position
    for piece, chunk in held:
        wait(piece, chunk, 1)
    yield
    for copy in copies:
        copy.wait_send()


def product(columns, counts, tiles, blocks, b):
    picked = []
    for s in range(SLOTS):
        name = columns[s, b]
        place = name // (COLS * BP) * BP + name % BP
        picked.append(blocks[jnp.where(s < counts[0, b], place, ROWS * BP)])
    vectors = jnp.concatenate(picked, axis=1)
    tile_row = jnp.concatenate([tiles[b, s] for s in range(SLOTS)], axis=1)
    return lax.dot_general(vectors, tile_row, (((1,), (1,)), ((), ())), preferred_element_type=F32)


def images(columns, counts, tiles, blocks, partial, arrived, send_sem, recv_sem):
    x, y, z, core = coords()
    col = lax.axis_index("col")

    def peer(offset):
        to_x, to_hi = lax.rem(x + offset, X), lax.rem(y // 2 + offset // X, 2)
        return to_hi * X + to_x, device(to_x, to_hi * 2 + lax.rem(y, 2), z, core)

    def copy(offset):
        owner, to = peer(offset)
        return remote(
            partial.at[pl.ds(owner * BP, BP)], arrived.at[offset], send_sem.at[offset], recv_sem.at[offset], to
        )

    def share(owner):
        return [product(columns, counts, tiles, blocks, owner * BP + within) for within in range(BP)]

    def send(offset):
        owner = peer(offset)[0]
        for within, image in enumerate(share(owner)):
            partial[owner * BP + within] = image.astype(partial.dtype)
        copy(offset).start()

    def step(i, carry):
        send(6 - i - 2 * (i // 2))
        send(7 - 3 * i + 2 * (i // 2))
        return carry

    lax.fori_loop(0, 3, step, 0)
    send(1)
    own = share(col)
    yield
    for offset in (6, 7, 5, 4, 2, 3, 1):
        copy(offset).wait_recv()
        for within in range(BP):
            own[within] = own[within] + arrived[offset, within].astype(F32)
    yield jnp.concatenate(own, axis=1)
    for offset in range(1, COLS):
        copy(offset).wait_send()


def sum_everywhere(gram, mine, other, plane, line, send_sem, recv_sem):
    x, y, z, core = coords()
    half = gram.shape[0] // 2
    mine[...] = jnp.concatenate([gram[:half], gram[half:]], axis=1)
    swap = remote(mine, other, send_sem.at[0], recv_sem.at[0], device(x, y, z, 1 - core))
    swap.start()
    yield
    swap.wait_recv()
    here = y * X + x
    plane[here] = mine[...] + other[...]

    def plane_copy(offset):
        to_x, to_y = lax.rem(x + offset, X), lax.rem(y + offset // X, Y)
        return remote(plane.at[here], plane.at[here], send_sem.at[offset], recv_sem.at[1 + here], device(to_x, to_y, z, core))

    def plane_from(offset):
        source = lax.rem(y + offset // X, Y) * X + lax.rem(x + offset, X)
        return remote(plane.at[source], plane.at[source], send_sem.at[offset], recv_sem.at[1 + source], device(x, y, z, 1 - core))

    for offset in PLANE_ORDER:
        plane_copy(offset).start()
    yield
    for offset in PLANE_ORDER:
        plane_from(offset).wait_recv()
    total = plane[0]
    for i in range(1, X * Y):
        total = total + plane[i]
    line[z] = total

    def line_copy(offset):
        return remote(
            line.at[z], line.at[z], send_sem.at[X * Y - 1 + offset], recv_sem.at[1 + X * Y + z], device(x, y, lax.rem(z + offset, Z), core)
        )

    def line_from(offset):
        source = lax.rem(z + offset, Z)
        return remote(
            line.at[source], line.at[source], send_sem.at[offset], recv_sem.at[1 + X * Y + source], device(x, y, z, 1 - core)
        )

    for offset in LINE_ORDER:
        line_copy(offset).start()
    yield
    for offset in range(1, Z):
        line_from(offset).wait_recv()
    total = line[0]
    for i in range(1, Z):
        total = total + line[i]
    vecs = gram.shape[1]
    yield jnp.concatenate([total[:, :vecs], total[:, vecs:]], axis=0)
    swap.wait_send()
    for offset in range(1, X * Y):
        plane_copy(offset).wait_send()
    for offset in range(1, Z):
        line_copy(offset).wait_send()


def factor(gram):
    n = gram.shape[0]
    shape = (n, 2 * n)
    rows, cols = lax.broadcasted_iota(jnp.int32, shape, 0), lax.broadcasted_iota(jnp.int32, shape, 1)
    work = jnp.concatenate([gram, jnp.where(cols == rows, 1.0, 0.0).astype(F32)[:, :n]], axis=1)
    span = range(PIVOTS)
    for j in range(0, n, PIVOTS):
        rest, below = work[j:], rows[j:]
        top = [rest[p : p + 1] for p in span]
        entry = {(p, q): jnp.broadcast_to(top[p][:, j + q : j + q + 1], top[p].shape) for p in span for q in span if q >= p}
        column = [jnp.broadcast_to(rest[:, j + p : j + p + 1], rest.shape) for p in span]
        for p in span:
            inverse = 1.0 / entry[p, p]
            rest = rest - jnp.where(below > j + p, column[p], 0.0) * (top[p] * inverse)
            for q in range(p + 1, PIVOTS):
                ratio = entry[p, q] * inverse
                top[q] = top[q] - ratio * top[p]
                column[q] = column[q] - ratio * column[p]
                for r in range(q, PIVOTS):
                    entry[q, r] = entry[q, r] - ratio * entry[p, r]
        work = jnp.concatenate([work[:j], rest], axis=0) if j else rest
    pivots = jnp.sum(jnp.where(rows == cols, work, 0.0), axis=1, keepdims=True)
    work = work * lax.rsqrt(pivots)
    upper = jnp.where(rows <= cols, work, 0.0)[:, :n]
    return upper, work[:, n:]


def advance(steps, count):
    for _ in range(count):
        next(steps)


def last(steps):
    result = None
    for result in steps:
        pass
    return result


def gram_of(image):
    return lax.dot_general(image, image, (((1,), (1,)), ((), ())), precision=HIGHEST, preferred_element_type=F32)


def growth(gram, inverse):
    diagonal = lax.broadcasted_iota(jnp.int32, gram.shape, 0) == lax.broadcasted_iota(jnp.int32, gram.shape, 1)
    lengths = jnp.sum(jnp.where(diagonal, gram, 0.0), axis=0, keepdims=True)
    return jnp.sum(inverse * (inverse * lengths)) / gram.shape[0], jnp.min(lengths), jnp.max(lengths)


def kernel(deferred, scaling, columns, counts, start_in, tiles_in, embedding, upper_out, *rest):
    flag, rest = (rest[0], rest[1:]) if deferred else (None, rest)
    (blocks_1, blocks_2, partial_1, partial_2, arrived_1, arrived_2, start, tiles, mine, other, plane, line,
     load_sem, gather_send, gather_recv, image_send, image_recv, sum_send, sum_recv) = rest
    x, y, z, core = coords()
    barrier = pltpu.get_barrier_semaphore()
    met = [device(x, y, z, 1 - core)]
    met += [device(lax.rem(x + o, X), lax.rem(y + o // X, Y), z, core) for o in range(1, X * Y)]
    met += [device(x, y, lax.rem(z + o, Z), core) for o in range(1, Z)]
    load_start = pltpu.make_async_copy(start_in, start, load_sem.at[0])
    load_start.start()
    for to in met:
        pl.semaphore_signal(barrier, inc=1, device_id=to, device_id_type=MESH)
    load = pltpu.make_async_copy(tiles_in, tiles, load_sem.at[1])
    load.start()

    vecs, size = start.shape[1:]
    row = lax.axis_index("row")
    for ref in (blocks_1, blocks_2):
        ref[ROWS * BP] = jnp.zeros((vecs, size), BF16)
    load_start.wait()
    blocks_1[pl.ds(row * BP, BP)] = start[...].astype(BF16)
    pl.semaphore_wait(barrier, len(met))

    def all_sum(it, gram):
        return sum_everywhere(
            gram, mine.at[it], other.at[it], plane.at[it], line.at[it], sum_send.at[it], sum_recv.at[it]
        )

    def gathered(it):
        return gather((blocks_1, blocks_2)[it], gather_send, gather_recv.at[it])

    def images_of(it):
        refs = ((blocks_1, partial_1, arrived_1), (blocks_2, partial_2, arrived_2))[it]
        return images(columns, counts, tiles, *refs, image_send, image_recv.at[it])

    def keep(image):
        for b in range(BP):
            blocks_2[row * BP + b] = image[:, b * size : (b + 1) * size].astype(BF16)

    pieces = gathered(0)
    advance(pieces, len(GATHER) + 1)
    load.wait()
    shares = images_of(0)
    next(shares)
    last(pieces)
    image = next(shares)

    if deferred:
        keep(image)
        pieces = gathered(1)
        next(pieces)
        last(shares)
        first_total = all_sum(0, gram_of(image))
        advance(first_total, 2)
        advance(pieces, len(GATHER))
        shares = images_of(1)
        next(shares)
        last(pieces)
        next(first_total)
        image = next(shares)
        total = all_sum(1, gram_of(image))
        advance(total, 2)
        last(shares)
        first_gram = next(first_total)
        last(first_total)
        _, first_inverse = factor(first_gram)
        first_growth, _, _ = growth(first_gram, first_inverse)
        advance(total, 1)
    else:
        last(shares)
        total = all_sum(0, gram_of(image))
        advance(total, 3)
        _, inverse = factor(next(total))
        last(total)
        keep(jnp.dot(inverse, image, precision=HIGHEST, preferred_element_type=F32))
        pieces = gathered(1)
        advance(pieces, len(GATHER) + 1)
        shares = images_of(1)
        next(shares)
        last(pieces)
        image = next(shares)
        last(shares)
        total = all_sum(1, gram_of(image))
        advance(total, 3)
    gram = next(total)

    upper, inverse = factor(gram)
    vectors = jnp.dot(inverse, image, precision=HIGHEST, preferred_element_type=F32)
    for b in range(BP):
        embedding[b] = vectors[:, b * size : (b + 1) * size] * scaling
    if deferred:
        upper = lax.dot_general(
            upper, first_inverse, (((1,), (1,)), ((), ())), precision=HIGHEST, preferred_element_type=F32
        )
        second_growth, least, most = growth(gram, inverse)
        safe = (first_growth < MAX_GROWTH) & (second_growth < MAX_GROWTH) & (least > 1e-18) & (most < 1e34)
        flag[0, 0] = safe.astype(jnp.int32)
    upper_out[...] = upper * (1.0 / scaling)
    last(total)


def call(deferred, affinity_tiles, columns, counts, start_vectors):
    rows = affinity_tiles.shape[0]
    pieces, vecs, size = start_vectors.shape
    scaling = math.sqrt(ROWS * COLS * BP * size)
    vmem, smem = pl.BlockSpec(memory_space=pltpu.VMEM), pl.BlockSpec(memory_space=pltpu.SMEM)
    hbm = pl.BlockSpec(memory_space=pl.ANY)
    dma = pltpu.SemaphoreType.DMA
    half = (vecs // 2, 2 * vecs)
    sent = [BF16 if deferred and narrow else F32 for narrow in NARROW]
    outs = [jax.ShapeDtypeStruct(start_vectors.shape, F32), jax.ShapeDtypeStruct((vecs, vecs), F32)]
    return pl.pallas_call(
        functools.partial(kernel, deferred, scaling),
        out_shape=outs + [jax.ShapeDtypeStruct((1, 1), jnp.int32)] * deferred,
        in_specs=[smem, smem, hbm, hbm],
        out_specs=[vmem, vmem] + [smem] * deferred,
        scratch_shapes=[pltpu.VMEM((ROWS * BP + 1, vecs, size), BF16)] * ITERS
        + [pltpu.VMEM((rows, vecs, size), dtype) for dtype in sent]
        + [pltpu.VMEM((COLS, pieces, vecs, size), dtype) for dtype in sent]
        + [
            pltpu.VMEM(start_vectors.shape, F32),
            pltpu.VMEM(affinity_tiles.shape, BF16),
            pltpu.VMEM((ITERS,) + half, F32),
            pltpu.VMEM((ITERS,) + half, F32),
            pltpu.VMEM((ITERS, X * Y) + half, F32),
            pltpu.VMEM((ITERS, Z) + half, F32),
            dma((2,)),
            dma((GATHER_SENDS,)),
            dma((ITERS, len(CHUNKS) * GATHER_SLOTS)),
            dma((COLS,)),
            dma((ITERS, COLS)),
            dma((ITERS, X * Y + Z)),
            dma((ITERS, 1 + X * Y + Z)),
        ],
        compiler_params=pltpu.CompilerParams(
            collective_id=int(deferred), has_side_effects=True, vmem_limit_bytes=48 * 1024 * 1024
        ),
        name="deferred" if deferred else "in_order",
    )(columns, counts, start_vectors, affinity_tiles)


def body(affinity_tiles, block_columns, slot_counts, start_vectors):
    args = (affinity_tiles, block_columns.T, slot_counts.T, start_vectors)
    embedding, upper, safe = call(True, *args)
    return lax.cond(safe[0, 0] > 0, lambda: (embedding, upper), lambda: tuple(call(False, *args)))


def solution(mesh):
    in_specs = (
        P("row", "col", None, None),
        P("row", "col"),
        P("row", "col"),
        P(("row", "col"), None, None),
    )
    out_specs = (P(("row", "col"), None, None), P())
    return jax.shard_map(body, mesh=mesh, in_specs=in_specs, out_specs=out_specs, check_vma=False)
```

```python
import functools
import math

import jax
import jax.numpy as jnp
from jax import lax
from jax.experimental import pallas as pl
from jax.experimental.pallas import tpu as pltpu
from jax.sharding import PartitionSpec as P

ITERS = 2
MESH = pl.DeviceIdType.MESH
F32 = jnp.float32
BF16 = jnp.bfloat16
HIGHEST = lax.Precision.HIGHEST
X, Y, Z = 4, 4, 8
COLS = 8
SLOTS = 8
BP = 4
ROWS = 32
PIVOTS = 8
MAX_GROWTH = 1.15
NARROW = (True, True)

CHUNKS = ((0, 4),)
GATHER = (
    ((0, 0), 0, (("z", 2), ("z", -2), ("y", 0), ("z", 1), ("z", -1), ("s", 0))),
    ((0, 6), 0, (("y", 0), ("z", 2), ("z", 1), ("s", 0))),
    ((0, 2), 0, (("y", 0), ("z", -1), ("s", 0))),
    ((0, 7), 0, (("y", 0), ("s", 0))),
    ((0, 1), 0, (("y", 0), ("s", 0))),
    ((1, 0), 0, (("s", 0),)),
    ((1, 6), 0, (("z", 1), ("z", 2), ("s", 0))),
    ((1, 2), 0, (("z", -1), ("s", 0))),
    ((1, 7), 0, (("s", 0),)),
    ((1, 1), 0, (("s", 0),)),
    ((0, 5), 0, (("s", 0),)),
    ((0, 3), 0, (("s", 0),)),
    ((1, 5), 0, (("s", 0),)),
    ((1, 3), 0, (("s", 0),)),
    ((0, 4), 0, (("s", 0),)),
    ((1, 4), 0, (("s", 0),)),
)
GATHER_SENDS = sum(len(targets) for _, _, targets in GATHER)
GATHER_SLOTS = 4 * Z

PLANE_ORDER = (10, 6, 9, 11, 14, 2, 5, 7, 8, 13, 15, 1, 3, 4, 12)
LINE_ORDER = (4, 3, 5, 2, 6, 1, 7)


def coords():
    row, col = lax.axis_index("row"), lax.axis_index("col")
    return lax.rem(col, 4), col // 4 * 2 + lax.rem(row // 2, 2), row // 4, lax.rem(row, 2)


def device(x, y, z, core):
    return (z * 4 + lax.rem(y, 2) * 2 + core, y // 2 * 4 + x)


def remote(src, dst, send_sem, recv_sem, to):
    return pltpu.make_async_remote_copy(
        src_ref=src, dst_ref=dst, send_sem=send_sem, recv_sem=recv_sem, device_id=to, device_id_type=MESH
    )


def gather(blocks, send_sem, recv_sem):
    x, y, z, core = coords()
    partner = y // 2 * 2 + 1 - lax.rem(y, 2)
    way = 1 - 2 * core

    def place(piece, chunk, core):
        column, dz = piece
        y_of = y if column == 0 else partner
        row = lax.rem(z + way * dz + Z, Z) * 4 + lax.rem(y_of, 2) * 2 + core
        return blocks.at[pl.ds(row * BP + CHUNKS[chunk][0], CHUNKS[chunk][1])]

    def slot(column, dz, chunk, other):
        return ((chunk * 2 + other) * 2 + column) * Z + dz

    def wait(piece, chunk, other):
        column, dz = piece
        here = place(piece, chunk, 1 - core if other else core)
        index = slot(column, -dz % Z if other else dz, chunk, other)
        remote(here, here, send_sem.at[0], recv_sem.at[index], device(x, y, z, 1 - core)).wait_recv()

    copies, held = [], [((0, 0), chunk) for chunk in range(len(CHUNKS))]
    for position, (piece, chunk, targets) in enumerate(GATHER):
        column, dz = piece
        if (piece, chunk) not in held:
            wait(piece, chunk, 0)
            held.append((piece, chunk))
        here = place(piece, chunk, core)
        for kind, step in targets:
            if kind == "z":
                to = device(x, y, lax.rem(z + way * step + Z, Z), core)
                index = slot(column, (dz - step) % Z, chunk, 0)
            elif kind == "y":
                to, index = device(x, partner, z, core), slot(1 - column, dz, chunk, 0)
            else:
                to, index = device(x, y, z, 1 - core), slot(column, dz, chunk, 1)
            copy = remote(here, here, send_sem.at[len(copies)], recv_sem.at[index], to)
            copy.start()
            copies.append(copy)
        yield position
    for piece, chunk in held:
        wait(piece, chunk, 1)
    yield
    for copy in copies:
        copy.wait_send()


def product(columns, counts, tiles, blocks, b):
    picked = []
    for s in range(SLOTS):
        name = columns[s, b]
        place = name // (COLS * BP) * BP + name % BP
        picked.append(blocks[jnp.where(s < counts[0, b], place, ROWS * BP)])
    vectors = jnp.concatenate(picked, axis=1)
    tile_row = jnp.concatenate([tiles[b, s] for s in range(SLOTS)], axis=1)
    return lax.dot_general(vectors, tile_row, (((1,), (1,)), ((), ())), preferred_element_type=F32)


def images(columns, counts, tiles, blocks, partial, arrived, send_sem, recv_sem):
    x, y, z, core = coords()
    col = lax.axis_index("col")

    def peer(offset):
        to_x, to_hi = lax.rem(x + offset, X), lax.rem(y // 2 + offset // X, 2)
        return to_hi * X + to_x, device(to_x, to_hi * 2 + lax.rem(y, 2), z, core)

    def copy(offset):
        owner, to = peer(offset)
        return remote(
            partial.at[pl.ds(owner * BP, BP)], arrived.at[offset], send_sem.at[offset], recv_sem.at[offset], to
        )

    def share(owner):
        return [product(columns, counts, tiles, blocks, owner * BP + within) for within in range(BP)]

    def send(offset):
        owner = peer(offset)[0]
        for within, image in enumerate(share(owner)):
            partial[owner * BP + within] = image.astype(partial.dtype)
        copy(offset).start()

    def step(i, carry):
        send(6 - i - 2 * (i // 2))
        send(7 - 3 * i + 2 * (i // 2))
        return carry

    lax.fori_loop(0, 3, step, 0)
    send(1)
    own = share(col)
    yield
    for offset in (6, 7, 5, 4, 2, 3, 1):
        copy(offset).wait_recv()
        for within in range(BP):
            own[within] = own[within] + arrived[offset, within].astype(F32)
    yield jnp.concatenate(own, axis=1)
    for offset in range(1, COLS):
        copy(offset).wait_send()


def sum_everywhere(gram, mine, other, plane, line, send_sem, recv_sem):
    x, y, z, core = coords()
    half = gram.shape[0] // 2

    def fold(square):
        return jnp.concatenate([square[i : i + 8] for i in range(0, half, 8)], axis=1)

    def unfold(flat):
        return jnp.concatenate([flat[:, i : i + half] for i in range(0, 4 * half, half)], axis=0)

    here = y * X + x
    plane[here] = jnp.concatenate([fold(gram[:half, :half]), fold(gram[:half, half:]), fold(gram[half:, half:])], axis=0)

    def plane_copy(offset):
        to_x, to_y = lax.rem(x + offset, X), lax.rem(y + offset // X, Y)
        return remote(plane.at[here], plane.at[here], send_sem.at[offset], recv_sem.at[1 + here], device(to_x, to_y, z, core))

    def plane_from(offset):
        source = lax.rem(y + offset // X, Y) * X + lax.rem(x + offset, X)
        return remote(plane.at[source], plane.at[source], send_sem.at[offset], recv_sem.at[1 + source], device(x, y, z, 1 - core))

    for offset in PLANE_ORDER:
        plane_copy(offset).start()
    yield
    for offset in PLANE_ORDER:
        plane_from(offset).wait_recv()
    total = plane[0]
    for i in range(1, X * Y):
        total = total + plane[i]
    line[z] = total

    def line_copy(offset):
        return remote(
            line.at[z], line.at[z], send_sem.at[X * Y - 1 + offset], recv_sem.at[1 + X * Y + z], device(x, y, lax.rem(z + offset, Z), core)
        )

    def line_from(offset):
        source = lax.rem(z + offset, Z)
        return remote(
            line.at[source], line.at[source], send_sem.at[offset], recv_sem.at[1 + X * Y + source], device(x, y, z, 1 - core)
        )

    for offset in LINE_ORDER:
        line_copy(offset).start()
    yield
    for offset in range(1, Z):
        line_from(offset).wait_recv()
    total = line[0]
    for i in range(1, Z):
        total = total + line[i]
    mine[...] = total
    swap = remote(mine, other, send_sem.at[0], recv_sem.at[0], device(x, y, z, 1 - core))
    swap.start()
    yield
    swap.wait_recv()
    total = mine[...] + other[...]
    first, cross, second = (unfold(total[i : i + 8]) for i in (0, 8, 16))
    yield jnp.concatenate(
        [jnp.concatenate([first, cross], axis=1), jnp.concatenate([cross.T, second], axis=1)], axis=0
    )
    swap.wait_send()
    for offset in range(1, X * Y):
        plane_copy(offset).wait_send()
    for offset in range(1, Z):
        line_copy(offset).wait_send()


def factor(gram):
    n = gram.shape[0]
    shape = (n, 2 * n)
    rows, cols = lax.broadcasted_iota(jnp.int32, shape, 0), lax.broadcasted_iota(jnp.int32, shape, 1)
    work = jnp.concatenate([gram, jnp.where(cols == rows, 1.0, 0.0).astype(F32)[:, :n]], axis=1)
    span = range(PIVOTS)
    for j in range(0, n, PIVOTS):
        rest, below = work[j:], rows[j:]
        top = [rest[p : p + 1] for p in span]
        entry = {(p, q): jnp.broadcast_to(top[p][:, j + q : j + q + 1], top[p].shape) for p in span for q in span if q >= p}
        column = [jnp.broadcast_to(rest[:, j + p : j + p + 1], rest.shape) for p in span]
        for p in span:
            inverse = 1.0 / entry[p, p]
            rest = rest - jnp.where(below > j + p, column[p], 0.0) * (top[p] * inverse)
            for q in range(p + 1, PIVOTS):
                ratio = entry[p, q] * inverse
                top[q] = top[q] - ratio * top[p]
                column[q] = column[q] - ratio * column[p]
                for r in range(q, PIVOTS):
                    entry[q, r] = entry[q, r] - ratio * entry[p, r]
        work = jnp.concatenate([work[:j], rest], axis=0) if j else rest
    pivots = jnp.sum(jnp.where(rows == cols, work, 0.0), axis=1, keepdims=True)
    work = work * lax.rsqrt(pivots)
    upper = jnp.where(rows <= cols, work, 0.0)[:, :n]
    return upper, work[:, n:]


def advance(steps, count):
    for _ in range(count):
        next(steps)


def last(steps):
    result = None
    for result in steps:
        pass
    return result


def gram_of(image):
    return lax.dot_general(image, image, (((1,), (1,)), ((), ())), precision=HIGHEST, preferred_element_type=F32)


def growth(gram, inverse):
    diagonal = lax.broadcasted_iota(jnp.int32, gram.shape, 0) == lax.broadcasted_iota(jnp.int32, gram.shape, 1)
    lengths = jnp.sum(jnp.where(diagonal, gram, 0.0), axis=0, keepdims=True)
    return jnp.sum(inverse * (inverse * lengths)) / gram.shape[0], jnp.min(lengths), jnp.max(lengths)


def kernel(deferred, scaling, columns, counts, start_in, tiles_in, embedding, upper_out, *rest):
    flag, rest = (rest[0], rest[1:]) if deferred else (None, rest)
    (blocks_1, blocks_2, partial_1, partial_2, arrived_1, arrived_2, start, tiles, mine, other, plane, line,
     load_sem, gather_send, gather_recv, image_send, image_recv, sum_send, sum_recv) = rest
    x, y, z, core = coords()
    barrier = pltpu.get_barrier_semaphore()
    met = [device(x, y, z, 1 - core)]
    met += [device(lax.rem(x + o, X), lax.rem(y + o // X, Y), z, core) for o in range(1, X * Y)]
    met += [device(x, y, lax.rem(z + o, Z), core) for o in range(1, Z)]
    load_start = pltpu.make_async_copy(start_in, start, load_sem.at[0])
    load_start.start()
    for to in met:
        pl.semaphore_signal(barrier, inc=1, device_id=to, device_id_type=MESH)
    load = pltpu.make_async_copy(tiles_in, tiles, load_sem.at[1])
    load.start()

    vecs, size = start.shape[1:]
    row = lax.axis_index("row")
    for ref in (blocks_1, blocks_2):
        ref[ROWS * BP] = jnp.zeros((vecs, size), BF16)
    load_start.wait()
    blocks_1[pl.ds(row * BP, BP)] = start[...].astype(BF16)
    pl.semaphore_wait(barrier, len(met))

    def all_sum(it, gram):
        return sum_everywhere(
            gram, mine.at[it], other.at[it], plane.at[it], line.at[it], sum_send.at[it], sum_recv.at[it]
        )

    def gathered(it):
        return gather((blocks_1, blocks_2)[it], gather_send, gather_recv.at[it])

    def images_of(it):
        refs = ((blocks_1, partial_1, arrived_1), (blocks_2, partial_2, arrived_2))[it]
        return images(columns, counts, tiles, *refs, image_send, image_recv.at[it])

    def keep(image):
        for b in range(BP):
            blocks_2[row * BP + b] = image[:, b * size : (b + 1) * size].astype(BF16)

    pieces = gathered(0)
    advance(pieces, len(GATHER) + 1)
    load.wait()
    shares = images_of(0)
    next(shares)
    last(pieces)
    image = next(shares)

    if deferred:
        keep(image)
        pieces = gathered(1)
        next(pieces)
        last(shares)
        first_total = all_sum(0, gram_of(image))
        next(first_total)
        advance(pieces, len(GATHER))
        shares = images_of(1)
        next(shares)
        last(pieces)
        next(first_total)
        image = next(shares)
        total = all_sum(1, gram_of(image))
        next(total)
        last(shares)
        next(first_total)
        first_gram = next(first_total)
        last(first_total)
        _, first_inverse = factor(first_gram)
        first_growth, _, _ = growth(first_gram, first_inverse)
        advance(total, 2)
    else:
        last(shares)
        total = all_sum(0, gram_of(image))
        advance(total, 3)
        _, inverse = factor(next(total))
        last(total)
        keep(jnp.dot(inverse, image, precision=HIGHEST, preferred_element_type=F32))
        pieces = gathered(1)
        advance(pieces, len(GATHER) + 1)
        shares = images_of(1)
        next(shares)
        last(pieces)
        image = next(shares)
        last(shares)
        total = all_sum(1, gram_of(image))
        advance(total, 3)
    gram = next(total)

    upper, inverse = factor(gram)
    vectors = jnp.dot(inverse, image, precision=HIGHEST, preferred_element_type=F32)
    for b in range(BP):
        embedding[b] = vectors[:, b * size : (b + 1) * size] * scaling
    if deferred:
        upper = lax.dot_general(
            upper, first_inverse, (((1,), (1,)), ((), ())), precision=HIGHEST, preferred_element_type=F32
        )
        second_growth, least, most = growth(gram, inverse)
        safe = (first_growth < MAX_GROWTH) & (second_growth < MAX_GROWTH) & (least > 1e-18) & (most < 1e34)
        flag[0, 0] = safe.astype(jnp.int32)
    upper_out[...] = upper * (1.0 / scaling)
    last(total)


def call(deferred, affinity_tiles, columns, counts, start_vectors):
    rows = affinity_tiles.shape[0]
    pieces, vecs, size = start_vectors.shape
    scaling = math.sqrt(ROWS * COLS * BP * size)
    vmem, smem = pl.BlockSpec(memory_space=pltpu.VMEM), pl.BlockSpec(memory_space=pltpu.SMEM)
    hbm = pl.BlockSpec(memory_space=pl.ANY)
    dma = pltpu.SemaphoreType.DMA
    half = (3 * vecs // 8, 2 * vecs)
    sent = [BF16 if deferred and narrow else F32 for narrow in NARROW]
    outs = [jax.ShapeDtypeStruct(start_vectors.shape, F32), jax.ShapeDtypeStruct((vecs, vecs), F32)]
    return pl.pallas_call(
        functools.partial(kernel, deferred, scaling),
        out_shape=outs + [jax.ShapeDtypeStruct((1, 1), jnp.int32)] * deferred,
        in_specs=[smem, smem, hbm, hbm],
        out_specs=[vmem, vmem] + [smem] * deferred,
        scratch_shapes=[pltpu.VMEM((ROWS * BP + 1, vecs, size), BF16)] * ITERS
        + [pltpu.VMEM((rows, vecs, size), dtype) for dtype in sent]
        + [pltpu.VMEM((COLS, pieces, vecs, size), dtype) for dtype in sent]
        + [
            pltpu.VMEM(start_vectors.shape, F32),
            pltpu.VMEM(affinity_tiles.shape, BF16),
            pltpu.VMEM((ITERS,) + half, F32),
            pltpu.VMEM((ITERS,) + half, F32),
            pltpu.VMEM((ITERS, X * Y) + half, F32),
            pltpu.VMEM((ITERS, Z) + half, F32),
            dma((2,)),
            dma((GATHER_SENDS,)),
            dma((ITERS, len(CHUNKS) * GATHER_SLOTS)),
            dma((COLS,)),
            dma((ITERS, COLS)),
            dma((ITERS, X * Y + Z)),
            dma((ITERS, 1 + X * Y + Z)),
        ],
        compiler_params=pltpu.CompilerParams(
            collective_id=int(deferred), has_side_effects=True, vmem_limit_bytes=48 * 1024 * 1024
        ),
        name="deferred" if deferred else "in_order",
    )(columns, counts, start_vectors, affinity_tiles)


def body(affinity_tiles, block_columns, slot_counts, start_vectors):
    args = (affinity_tiles, block_columns.T, slot_counts.T, start_vectors)
    embedding, upper, safe = call(True, *args)
    return lax.cond(safe[0, 0] > 0, lambda: (embedding, upper), lambda: tuple(call(False, *args)))


def solution(mesh):
    in_specs = (
        P("row", "col", None, None),
        P("row", "col"),
        P("row", "col"),
        P(("row", "col"), None, None),
    )
    out_specs = (P(("row", "col"), None, None), P())
    return jax.shard_map(body, mesh=mesh, in_specs=in_specs, out_specs=out_specs, check_vma=False)
```

```python
import functools
import math

import jax
import jax.numpy as jnp
from jax import lax
from jax.experimental import pallas as pl
from jax.experimental.pallas import tpu as pltpu
from jax.sharding import PartitionSpec as P

ITERS = 2
MESH = pl.DeviceIdType.MESH
F32 = jnp.float32
BF16 = jnp.bfloat16
HIGHEST = lax.Precision.HIGHEST
X, Y, Z = 4, 4, 8
COLS = 8
SLOTS = 8
BP = 4
ROWS = 32
PIVOTS = 8
MAX_GROWTH = 1.15
NARROW = (True, True)

CHUNKS = ((0, 4),)
GATHER = (
    ((0, 0), 0, (("z", 2), ("z", -2), ("y", 0), ("z", 1), ("z", -1), ("s", 0))),
    ((0, 6), 0, (("y", 0), ("z", 2), ("z", 1), ("s", 0))),
    ((0, 2), 0, (("y", 0), ("z", -1), ("s", 0))),
    ((0, 7), 0, (("y", 0), ("s", 0))),
    ((0, 1), 0, (("y", 0), ("s", 0))),
    ((1, 0), 0, (("s", 0),)),
    ((1, 6), 0, (("z", 1), ("z", 2), ("s", 0))),
    ((1, 2), 0, (("z", -1), ("s", 0))),
    ((1, 7), 0, (("s", 0),)),
    ((1, 1), 0, (("s", 0),)),
    ((0, 5), 0, (("s", 0),)),
    ((0, 3), 0, (("s", 0),)),
    ((1, 5), 0, (("s", 0),)),
    ((1, 3), 0, (("s", 0),)),
    ((0, 4), 0, (("s", 0),)),
    ((1, 4), 0, (("s", 0),)),
)
GATHER_SENDS = sum(len(targets) for _, _, targets in GATHER)
GATHER_SLOTS = 4 * Z

SUM_SLOTS = 2 + X * Y + Z


def coords():
    row, col = lax.axis_index("row"), lax.axis_index("col")
    return lax.rem(col, 4), col // 4 * 2 + lax.rem(row // 2, 2), row // 4, lax.rem(row, 2)


def device(x, y, z, core):
    return (z * 4 + lax.rem(y, 2) * 2 + core, y // 2 * 4 + x)


def remote(src, dst, send_sem, recv_sem, to):
    return pltpu.make_async_remote_copy(
        src_ref=src, dst_ref=dst, send_sem=send_sem, recv_sem=recv_sem, device_id=to, device_id_type=MESH
    )


def gather(blocks, send_sem, recv_sem):
    x, y, z, core = coords()
    partner = y // 2 * 2 + 1 - lax.rem(y, 2)
    way = 1 - 2 * core

    def place(piece, chunk, core):
        column, dz = piece
        y_of = y if column == 0 else partner
        row = lax.rem(z + way * dz + Z, Z) * 4 + lax.rem(y_of, 2) * 2 + core
        return blocks.at[pl.ds(row * BP + CHUNKS[chunk][0], CHUNKS[chunk][1])]

    def slot(column, dz, chunk, other):
        return ((chunk * 2 + other) * 2 + column) * Z + dz

    def wait(piece, chunk, other):
        column, dz = piece
        here = place(piece, chunk, 1 - core if other else core)
        index = slot(column, -dz % Z if other else dz, chunk, other)
        remote(here, here, send_sem.at[0], recv_sem.at[index], device(x, y, z, 1 - core)).wait_recv()

    copies, held = [], [((0, 0), chunk) for chunk in range(len(CHUNKS))]
    for position, (piece, chunk, targets) in enumerate(GATHER):
        column, dz = piece
        if (piece, chunk) not in held:
            wait(piece, chunk, 0)
            held.append((piece, chunk))
        here = place(piece, chunk, core)
        for kind, step in targets:
            if kind == "z":
                to = device(x, y, lax.rem(z + way * step + Z, Z), core)
                index = slot(column, (dz - step) % Z, chunk, 0)
            elif kind == "y":
                to, index = device(x, partner, z, core), slot(1 - column, dz, chunk, 0)
            else:
                to, index = device(x, y, z, 1 - core), slot(column, dz, chunk, 1)
            copy = remote(here, here, send_sem.at[len(copies)], recv_sem.at[index], to)
            copy.start()
            copies.append(copy)
        yield position
    for piece, chunk in held:
        wait(piece, chunk, 1)
    yield
    for copy in copies:
        copy.wait_send()


def product(columns, counts, tiles, blocks, b):
    picked = []
    for s in range(SLOTS):
        name = columns[s, b]
        place = name // (COLS * BP) * BP + name % BP
        picked.append(blocks[jnp.where(s < counts[0, b], place, ROWS * BP)])
    vectors = jnp.concatenate(picked, axis=1)
    tile_row = jnp.concatenate([tiles[b, s] for s in range(SLOTS)], axis=1)
    return lax.dot_general(vectors, tile_row, (((1,), (1,)), ((), ())), preferred_element_type=F32)


def images(columns, counts, tiles, blocks, partial, arrived, send_sem, recv_sem):
    x, y, z, core = coords()
    col = lax.axis_index("col")

    def peer(offset):
        to_x, to_hi = lax.rem(x + offset, X), lax.rem(y // 2 + offset // X, 2)
        return to_hi * X + to_x, device(to_x, to_hi * 2 + lax.rem(y, 2), z, core)

    def copy(offset):
        owner, to = peer(offset)
        return remote(
            partial.at[pl.ds(owner * BP, BP)], arrived.at[offset], send_sem.at[offset], recv_sem.at[offset], to
        )

    def share(owner):
        return [product(columns, counts, tiles, blocks, owner * BP + within) for within in range(BP)]

    def send(offset):
        owner = peer(offset)[0]
        for within, image in enumerate(share(owner)):
            partial[owner * BP + within] = image.astype(partial.dtype)
        copy(offset).start()

    def step(i, carry):
        send(6 - i - 2 * (i // 2))
        send(7 - 3 * i + 2 * (i // 2))
        return carry

    lax.fori_loop(0, 3, step, 0)
    send(1)
    own = share(col)
    yield
    for offset in (6, 7, 5, 4, 2, 3, 1):
        copy(offset).wait_recv()
        for within in range(BP):
            own[within] = own[within] + arrived[offset, within].astype(F32)
    yield jnp.concatenate(own, axis=1)
    for offset in range(1, COLS):
        copy(offset).wait_send()


def stages(lines):
    x, y, z, core = coords()
    cores = (2, core, lambda o: device(x, y, z, 1 - core), lambda o: 1 - core, (1,))
    along_z = (
        Z,
        z,
        lambda o: device(x, y, lax.rem(z + o, Z), core),
        lambda o: lax.rem(z + o, Z),
        (4, 3, 5, 2, 6, 1, 7),
    )
    if lines:
        along_x = (X, x, lambda o: device(lax.rem(x + o, X), y, z, core), lambda o: lax.rem(x + o, X), (2, 1, 3))
        along_y = (Y, y, lambda o: device(x, lax.rem(y + o, Y), z, core), lambda o: lax.rem(y + o, Y), (2, 1, 3))
        return cores, along_x, along_y, along_z
    plane = (
        X * Y,
        y * X + x,
        lambda o: device(lax.rem(x + o, X), lax.rem(y + o // X, Y), z, core),
        lambda o: lax.rem(y + o // X, Y) * X + lax.rem(x + o, X),
        (10, 6, 9, 11, 14, 2, 5, 7, 8, 13, 15, 1, 3, 4, 12),
    )
    return cores, plane, along_z


def sum_everywhere(gram, lines, parts, send_sem, recv_sem):
    x, y, z, core = coords()
    half = gram.shape[0] // 2

    def fold(square):
        return jnp.concatenate([square[i : i + 8] for i in range(0, half, 8)], axis=1)

    def unfold(flat):
        return jnp.concatenate([flat[:, i : i + half] for i in range(0, 4 * half, half)], axis=0)

    total = jnp.concatenate([fold(gram[:half, :half]), fold(gram[:half, half:]), fold(gram[half:, half:])], axis=0)
    base, copies = 0, []
    for count, mine, to, source, order in stages(lines):
        here = parts.at[base + mine]
        here[...] = total
        for offset in order:
            copy = remote(here, here, send_sem.at[base + offset], recv_sem.at[base + mine], to(offset))
            copy.start()
            copies.append(copy)
        yield
        for offset in order:
            there = parts.at[base + source(offset)]
            arrival = recv_sem.at[base + source(offset)]
            remote(there, there, send_sem.at[0], arrival, device(x, y, z, 1 - core)).wait_recv()
        total = parts[base]
        for i in range(1, count):
            total = total + parts[base + i]
        base += count
    first, cross, second = (unfold(total[i : i + 8]) for i in (0, 8, 16))
    yield jnp.concatenate(
        [jnp.concatenate([first, cross], axis=1), jnp.concatenate([cross.T, second], axis=1)], axis=0
    )
    for copy in copies:
        copy.wait_send()


def factor(gram):
    n = gram.shape[0]
    shape = (n, 2 * n)
    rows, cols = lax.broadcasted_iota(jnp.int32, shape, 0), lax.broadcasted_iota(jnp.int32, shape, 1)
    work = jnp.concatenate([gram, jnp.where(cols == rows, 1.0, 0.0).astype(F32)[:, :n]], axis=1)
    span = range(PIVOTS)
    for j in range(0, n, PIVOTS):
        rest, below = work[j:], rows[j:]
        top = [rest[p : p + 1] for p in span]
        entry = {(p, q): jnp.broadcast_to(top[p][:, j + q : j + q + 1], top[p].shape) for p in span for q in span if q >= p}
        column = [jnp.broadcast_to(rest[:, j + p : j + p + 1], rest.shape) for p in span]
        for p in span:
            inverse = 1.0 / entry[p, p]
            rest = rest - jnp.where(below > j + p, column[p], 0.0) * (top[p] * inverse)
            for q in range(p + 1, PIVOTS):
                ratio = entry[p, q] * inverse
                top[q] = top[q] - ratio * top[p]
                column[q] = column[q] - ratio * column[p]
                for r in range(q, PIVOTS):
                    entry[q, r] = entry[q, r] - ratio * entry[p, r]
        work = jnp.concatenate([work[:j], rest], axis=0) if j else rest
    pivots = jnp.sum(jnp.where(rows == cols, work, 0.0), axis=1, keepdims=True)
    work = work * lax.rsqrt(pivots)
    upper = jnp.where(rows <= cols, work, 0.0)[:, :n]
    return upper, work[:, n:]


def advance(steps, count):
    for _ in range(count):
        next(steps)


def last(steps):
    result = None
    for result in steps:
        pass
    return result


def gram_of(image):
    return lax.dot_general(image, image, (((1,), (1,)), ((), ())), precision=HIGHEST, preferred_element_type=F32)


def growth(gram, inverse):
    diagonal = lax.broadcasted_iota(jnp.int32, gram.shape, 0) == lax.broadcasted_iota(jnp.int32, gram.shape, 1)
    lengths = jnp.sum(jnp.where(diagonal, gram, 0.0), axis=0, keepdims=True)
    return jnp.sum(inverse * (inverse * lengths)) / gram.shape[0], jnp.min(lengths), jnp.max(lengths)


def kernel(deferred, scaling, columns, counts, start_in, tiles_in, embedding, upper_out, *rest):
    flag, rest = (rest[0], rest[1:]) if deferred else (None, rest)
    (blocks_1, blocks_2, partial_1, partial_2, arrived_1, arrived_2, start, tiles, parts_1, parts_2,
     load_sem, gather_send, gather_recv, image_send, image_recv, sum_send, sum_recv, known) = rest
    x, y, z, core = coords()
    barrier = pltpu.get_barrier_semaphore()
    beside_x = [device(lax.rem(x + o, X), y, z, core) for o in (1, X - 1)]
    met = [device(x, y, z, 1 - core)] + beside_x
    met += [device(x, lax.rem(y + o, Y), z, core) for o in (1, Y - 1)]
    met += [device(x, y, lax.rem(z + o, Z), core) for o in (1, 2, Z - 2, Z - 1)]
    load_start = pltpu.make_async_copy(start_in, start, load_sem.at[0])
    load_start.start()
    for to in met:
        pl.semaphore_signal(barrier, inc=1, device_id=to, device_id_type=MESH)
    load = pltpu.make_async_copy(tiles_in, tiles, load_sem.at[1])
    load.start()

    vecs, size = start.shape[1:]
    row = lax.axis_index("row")
    for ref in (blocks_1, blocks_2):
        ref[ROWS * BP] = jnp.zeros((vecs, size), BF16)
    load_start.wait()
    blocks_1[pl.ds(row * BP, BP)] = start[...].astype(BF16)
    pl.semaphore_wait(barrier, len(met))

    def all_sum(it, gram):
        lines = deferred and it == 0
        return sum_everywhere(gram, lines, (parts_1, parts_2)[it], sum_send.at[it], sum_recv.at[it])

    def gathered(it):
        return gather((blocks_1, blocks_2)[it], gather_send, gather_recv.at[it])

    def images_of(it):
        refs = ((blocks_1, partial_1, arrived_1), (blocks_2, partial_2, arrived_2))[it]
        return images(columns, counts, tiles, *refs, image_send, image_recv.at[it])

    def keep(image):
        for b in range(BP):
            blocks_2[row * BP + b] = image[:, b * size : (b + 1) * size].astype(BF16)

    def tell_beside_x(turn):
        for to in beside_x:
            pl.semaphore_signal(known.at[turn], inc=1, device_id=to, device_id_type=MESH)

    pieces = gathered(0)
    advance(pieces, 6)
    tell_beside_x(0)
    advance(pieces, 7)
    pl.semaphore_wait(known.at[0], 2)
    tell_beside_x(1)
    advance(pieces, len(GATHER) + 1 - 13)
    load.wait()
    pl.semaphore_wait(known.at[1], 2)
    shares = images_of(0)
    next(shares)
    last(pieces)
    image = next(shares)

    if deferred:
        keep(image)
        pieces = gathered(1)
        next(pieces)
        last(shares)
        first_total = all_sum(0, gram_of(image))
        next(first_total)
        advance(pieces, len(GATHER))
        next(first_total)
        shares = images_of(1)
        next(shares)
        last(pieces)
        next(first_total)
        image = next(shares)
        total = all_sum(1, gram_of(image))
        advance(total, 2)
        next(first_total)
        last(shares)
        next(total)
        first_gram = next(first_total)
        last(first_total)
        _, first_inverse = factor(first_gram)
        first_growth, _, _ = growth(first_gram, first_inverse)
    else:
        last(shares)
        total = all_sum(0, gram_of(image))
        advance(total, 3)
        _, inverse = factor(next(total))
        last(total)
        keep(jnp.dot(inverse, image, precision=HIGHEST, preferred_element_type=F32))
        pieces = gathered(1)
        advance(pieces, len(GATHER) + 1)
        shares = images_of(1)
        next(shares)
        last(pieces)
        image = next(shares)
        last(shares)
        total = all_sum(1, gram_of(image))
        advance(total, 3)
    gram = next(total)

    upper, inverse = factor(gram)
    vectors = jnp.dot(inverse, image, precision=HIGHEST, preferred_element_type=F32)
    for b in range(BP):
        embedding[b] = vectors[:, b * size : (b + 1) * size] * scaling
    if deferred:
        upper = lax.dot_general(
            upper, first_inverse, (((1,), (1,)), ((), ())), precision=HIGHEST, preferred_element_type=F32
        )
        second_growth, least, most = growth(gram, inverse)
        safe = (first_growth < MAX_GROWTH) & (second_growth < MAX_GROWTH) & (least > 1e-18) & (most < 1e34)
        flag[0, 0] = safe.astype(jnp.int32)
    upper_out[...] = upper * (1.0 / scaling)
    last(total)


def call(deferred, affinity_tiles, columns, counts, start_vectors):
    rows = affinity_tiles.shape[0]
    pieces, vecs, size = start_vectors.shape
    scaling = math.sqrt(ROWS * COLS * BP * size)
    vmem, smem = pl.BlockSpec(memory_space=pltpu.VMEM), pl.BlockSpec(memory_space=pltpu.SMEM)
    hbm = pl.BlockSpec(memory_space=pl.ANY)
    dma = pltpu.SemaphoreType.DMA
    sent = [BF16 if deferred and narrow else F32 for narrow in NARROW]
    outs = [jax.ShapeDtypeStruct(start_vectors.shape, F32), jax.ShapeDtypeStruct((vecs, vecs), F32)]
    return pl.pallas_call(
        functools.partial(kernel, deferred, scaling),
        out_shape=outs + [jax.ShapeDtypeStruct((1, 1), jnp.int32)] * deferred,
        in_specs=[smem, smem, hbm, hbm],
        out_specs=[vmem, vmem] + [smem] * deferred,
        scratch_shapes=[pltpu.VMEM((ROWS * BP + 1, vecs, size), BF16)] * ITERS
        + [pltpu.VMEM((rows, vecs, size), dtype) for dtype in sent]
        + [pltpu.VMEM((COLS, pieces, vecs, size), dtype) for dtype in sent]
        + [
            pltpu.VMEM(start_vectors.shape, F32),
            pltpu.VMEM(affinity_tiles.shape, BF16),
            pltpu.VMEM((SUM_SLOTS, 3 * vecs // 8, 2 * vecs), F32),
            pltpu.VMEM((SUM_SLOTS, 3 * vecs // 8, 2 * vecs), F32),
            dma((2,)),
            dma((GATHER_SENDS,)),
            dma((ITERS, len(CHUNKS) * GATHER_SLOTS)),
            dma((COLS,)),
            dma((ITERS, COLS)),
            dma((ITERS, SUM_SLOTS)),
            dma((ITERS, SUM_SLOTS)),
            pltpu.SemaphoreType.REGULAR((2,)),
        ],
        compiler_params=pltpu.CompilerParams(
            collective_id=int(deferred), has_side_effects=True, vmem_limit_bytes=48 * 1024 * 1024
        ),
        name="deferred" if deferred else "in_order",
    )(columns, counts, start_vectors, affinity_tiles)


def body(affinity_tiles, block_columns, slot_counts, start_vectors):
    args = (affinity_tiles, block_columns.T, slot_counts.T, start_vectors)
    embedding, upper, safe = call(True, *args)
    return lax.cond(safe[0, 0] > 0, lambda: (embedding, upper), lambda: tuple(call(False, *args)))


def solution(mesh):
    in_specs = (
        P("row", "col", None, None),
        P("row", "col"),
        P("row", "col"),
        P(("row", "col"), None, None),
    )
    out_specs = (P(("row", "col"), None, None), P())
    return jax.shard_map(body, mesh=mesh, in_specs=in_specs, out_specs=out_specs, check_vma=False)
```

```python
import functools
import math

import jax
import jax.numpy as jnp
from jax import lax
from jax.experimental import pallas as pl
from jax.experimental.pallas import tpu as pltpu
from jax.sharding import PartitionSpec as P

ITERS = 2
MESH = pl.DeviceIdType.MESH
F32 = jnp.float32
BF16 = jnp.bfloat16
HIGHEST = lax.Precision.HIGHEST
X, Y, Z = 4, 4, 8
COLS = 8
SLOTS = 8
BP = 4
ROWS = 32
PIVOTS = 8
MAX_GROWTH = 1.15
NARROW = (True, True)

CHUNKS = ((0, 4),)
GATHER = (
    ((0, 0), 0, (("z", 2), ("z", -2), ("y", 0), ("z", 1), ("z", -1), ("s", 0))),
    ((0, 6), 0, (("y", 0), ("z", 2), ("z", 1), ("s", 0))),
    ((0, 2), 0, (("y", 0), ("z", -1), ("s", 0))),
    ((0, 7), 0, (("y", 0), ("s", 0))),
    ((0, 1), 0, (("y", 0), ("s", 0))),
    ((1, 0), 0, (("s", 0),)),
    ((1, 6), 0, (("z", 1), ("z", 2), ("s", 0))),
    ((1, 2), 0, (("z", -1), ("s", 0))),
    ((1, 7), 0, (("s", 0),)),
    ((1, 1), 0, (("s", 0),)),
    ((0, 5), 0, (("s", 0),)),
    ((0, 3), 0, (("s", 0),)),
    ((1, 5), 0, (("s", 0),)),
    ((1, 3), 0, (("s", 0),)),
    ((0, 4), 0, (("s", 0),)),
    ((1, 4), 0, (("s", 0),)),
)
GATHER_SENDS = sum(len(targets) for _, _, targets in GATHER)
GATHER_SLOTS = 4 * Z

SUM_SLOTS = 2 + X * Y + Z


def coords():
    row, col = lax.axis_index("row"), lax.axis_index("col")
    return lax.rem(col, 4), col // 4 * 2 + lax.rem(row // 2, 2), row // 4, lax.rem(row, 2)


def device(x, y, z, core):
    return (z * 4 + lax.rem(y, 2) * 2 + core, y // 2 * 4 + x)


def remote(src, dst, send_sem, recv_sem, to):
    return pltpu.make_async_remote_copy(
        src_ref=src, dst_ref=dst, send_sem=send_sem, recv_sem=recv_sem, device_id=to, device_id_type=MESH
    )


def gather(blocks, send_sem, recv_sem):
    x, y, z, core = coords()
    partner = y // 2 * 2 + 1 - lax.rem(y, 2)
    way = 1 - 2 * core

    def place(piece, chunk, core):
        column, dz = piece
        y_of = y if column == 0 else partner
        row = lax.rem(z + way * dz + Z, Z) * 4 + lax.rem(y_of, 2) * 2 + core
        return blocks.at[pl.ds(row * BP + CHUNKS[chunk][0], CHUNKS[chunk][1])]

    def slot(column, dz, chunk, other):
        return ((chunk * 2 + other) * 2 + column) * Z + dz

    def wait(piece, chunk, other):
        column, dz = piece
        here = place(piece, chunk, 1 - core if other else core)
        index = slot(column, -dz % Z if other else dz, chunk, other)
        remote(here, here, send_sem.at[0], recv_sem.at[index], device(x, y, z, 1 - core)).wait_recv()

    copies, held = [], [((0, 0), chunk) for chunk in range(len(CHUNKS))]
    for position, (piece, chunk, targets) in enumerate(GATHER):
        column, dz = piece
        if (piece, chunk) not in held:
            wait(piece, chunk, 0)
            held.append((piece, chunk))
        here = place(piece, chunk, core)
        for kind, step in targets:
            if kind == "z":
                to = device(x, y, lax.rem(z + way * step + Z, Z), core)
                index = slot(column, (dz - step) % Z, chunk, 0)
            elif kind == "y":
                to, index = device(x, partner, z, core), slot(1 - column, dz, chunk, 0)
            else:
                to, index = device(x, y, z, 1 - core), slot(column, dz, chunk, 1)
            copy = remote(here, here, send_sem.at[len(copies)], recv_sem.at[index], to)
            copy.start()
            copies.append(copy)
        yield position
    for piece, chunk in held:
        wait(piece, chunk, 1)
    yield
    for copy in copies:
        copy.wait_send()


def product(columns, counts, tiles, blocks, b):
    picked = []
    for s in range(SLOTS):
        name = columns[s, b]
        place = name // (COLS * BP) * BP + name % BP
        picked.append(blocks[jnp.where(s < counts[0, b], place, ROWS * BP)])
    vectors = jnp.concatenate(picked, axis=1)
    tile_row = jnp.concatenate([tiles[b, s] for s in range(SLOTS)], axis=1)
    return lax.dot_general(vectors, tile_row, (((1,), (1,)), ((), ())), preferred_element_type=F32)


def images(columns, counts, tiles, blocks, partial, arrived, send_sem, recv_sem):
    x, y, z, core = coords()
    col = lax.axis_index("col")

    def peer(offset):
        to_x, to_hi = lax.rem(x + offset, X), lax.rem(y // 2 + offset // X, 2)
        return to_hi * X + to_x, device(to_x, to_hi * 2 + lax.rem(y, 2), z, core)

    def copy(offset):
        owner, to = peer(offset)
        return remote(
            partial.at[pl.ds(owner * BP, BP)], arrived.at[offset], send_sem.at[offset], recv_sem.at[offset], to
        )

    def share(owner):
        return [product(columns, counts, tiles, blocks, owner * BP + within) for within in range(BP)]

    def send(offset):
        owner = peer(offset)[0]
        for within, image in enumerate(share(owner)):
            partial[owner * BP + within] = image.astype(partial.dtype)
        copy(offset).start()

    def step(i, carry):
        send(6 - i - 2 * (i // 2))
        send(7 - 3 * i + 2 * (i // 2))
        return carry

    lax.fori_loop(0, 3, step, 0)
    send(1)
    own = share(col)
    yield
    for offset in (6, 7, 5, 4, 2, 3, 1):
        copy(offset).wait_recv()
        for within in range(BP):
            own[within] = own[within] + arrived[offset, within].astype(F32)
    yield jnp.concatenate(own, axis=1)
    for offset in range(1, COLS):
        copy(offset).wait_send()


def stages(lines):
    x, y, z, core = coords()
    cores = (2, core, lambda o: device(x, y, z, 1 - core), lambda o: 1 - core, (1,))
    along_z = (
        Z,
        z,
        lambda o: device(x, y, lax.rem(z + o, Z), core),
        lambda o: lax.rem(z + o, Z),
        (4, 3, 5, 2, 6, 1, 7),
    )
    if lines:
        along_x = (X, x, lambda o: device(lax.rem(x + o, X), y, z, core), lambda o: lax.rem(x + o, X), (2, 1, 3))
        along_y = (Y, y, lambda o: device(x, lax.rem(y + o, Y), z, core), lambda o: lax.rem(y + o, Y), (2, 1, 3))
        return cores, along_x, along_y, along_z
    plane = (
        X * Y,
        y * X + x,
        lambda o: device(lax.rem(x + o, X), lax.rem(y + o // X, Y), z, core),
        lambda o: lax.rem(y + o // X, Y) * X + lax.rem(x + o, X),
        (10, 6, 9, 11, 14, 2, 5, 7, 8, 13, 15, 1, 3, 4, 12),
    )
    return cores, plane, along_z


def sum_everywhere(gram, lines, parts, send_sem, recv_sem):
    x, y, z, core = coords()
    half = gram.shape[0] // 2

    def fold(square):
        return jnp.concatenate([square[i : i + 8] for i in range(0, half, 8)], axis=1)

    def unfold(flat):
        return jnp.concatenate([flat[:, i : i + half] for i in range(0, 4 * half, half)], axis=0)

    total = jnp.concatenate([fold(gram[:half, :half]), fold(gram[:half, half:]), fold(gram[half:, half:])], axis=0)
    base, copies = 0, []
    for count, mine, to, source, order in stages(lines):
        sent, copies = copies, []
        here = parts.at[base + mine]
        here[...] = total
        for offset in order:
            copy = remote(here, here, send_sem.at[base + offset], recv_sem.at[base + mine], to(offset))
            copy.start()
            copies.append(copy)
        yield
        for copy in sent:
            copy.wait_send()
        for offset in order:
            there = parts.at[base + source(offset)]
            arrival = recv_sem.at[base + source(offset)]
            remote(there, there, send_sem.at[0], arrival, device(x, y, z, 1 - core)).wait_recv()
        total = parts[base]
        for i in range(1, count):
            total = total + parts[base + i]
        base += count
    first, cross, second = (unfold(total[i : i + 8]) for i in (0, 8, 16))
    yield jnp.concatenate(
        [jnp.concatenate([first, cross], axis=1), jnp.concatenate([cross.T, second], axis=1)], axis=0
    )
    for copy in copies:
        copy.wait_send()


def factor(gram):
    n = gram.shape[0]
    shape = (n, 2 * n)
    rows, cols = lax.broadcasted_iota(jnp.int32, shape, 0), lax.broadcasted_iota(jnp.int32, shape, 1)
    work = jnp.concatenate([gram, jnp.where(cols == rows, 1.0, 0.0).astype(F32)[:, :n]], axis=1)
    span = range(PIVOTS)
    for j in range(0, n, PIVOTS):
        rest, below = work[j:], rows[j:]
        top = [rest[p : p + 1] for p in span]
        entry = {(p, q): jnp.broadcast_to(top[p][:, j + q : j + q + 1], top[p].shape) for p in span for q in span if q >= p}
        column = [jnp.broadcast_to(rest[:, j + p : j + p + 1], rest.shape) for p in span]
        for p in span:
            inverse = 1.0 / entry[p, p]
            rest = rest - jnp.where(below > j + p, column[p], 0.0) * (top[p] * inverse)
            for q in range(p + 1, PIVOTS):
                ratio = entry[p, q] * inverse
                top[q] = top[q] - ratio * top[p]
                column[q] = column[q] - ratio * column[p]
                for r in range(q, PIVOTS):
                    entry[q, r] = entry[q, r] - ratio * entry[p, r]
        work = jnp.concatenate([work[:j], rest], axis=0) if j else rest
    pivots = jnp.sum(jnp.where(rows == cols, work, 0.0), axis=1, keepdims=True)
    work = work * lax.rsqrt(pivots)
    upper = jnp.where(rows <= cols, work, 0.0)[:, :n]
    return upper, work[:, n:]


def advance(steps, count):
    for _ in range(count):
        next(steps)


def last(steps):
    result = None
    for result in steps:
        pass
    return result


def gram_of(image):
    return lax.dot_general(image, image, (((1,), (1,)), ((), ())), precision=HIGHEST, preferred_element_type=F32)


def growth(gram, inverse):
    diagonal = lax.broadcasted_iota(jnp.int32, gram.shape, 0) == lax.broadcasted_iota(jnp.int32, gram.shape, 1)
    lengths = jnp.sum(jnp.where(diagonal, gram, 0.0), axis=0, keepdims=True)
    return jnp.sum(inverse * (inverse * lengths)) / gram.shape[0], jnp.min(lengths), jnp.max(lengths)


def kernel(deferred, scaling, columns, counts, start_in, tiles_in, embedding, upper_out, *rest):
    flag, rest = (rest[0], rest[1:]) if deferred else (None, rest)
    (blocks_1, blocks_2, partial_1, partial_2, arrived_1, arrived_2, start, tiles, parts_1, parts_2,
     load_sem, gather_send, gather_recv, image_send, image_recv, sum_send, sum_recv, known) = rest
    x, y, z, core = coords()
    barrier = pltpu.get_barrier_semaphore()
    beside_x = [device(lax.rem(x + o, X), y, z, core) for o in (1, X - 1)]
    met = [device(x, y, z, 1 - core)] + beside_x
    met += [device(x, lax.rem(y + o, Y), z, core) for o in (1, Y - 1)]
    met += [device(x, y, lax.rem(z + o, Z), core) for o in (1, 2, Z - 2, Z - 1)]
    load_start = pltpu.make_async_copy(start_in, start, load_sem.at[0])
    load_start.start()
    for to in met:
        pl.semaphore_signal(barrier, inc=1, device_id=to, device_id_type=MESH)
    load = pltpu.make_async_copy(tiles_in, tiles, load_sem.at[1])
    load.start()

    vecs, size = start.shape[1:]
    row = lax.axis_index("row")
    for ref in (blocks_1, blocks_2):
        ref[ROWS * BP] = jnp.zeros((vecs, size), BF16)
    load_start.wait()
    blocks_1[pl.ds(row * BP, BP)] = start[...].astype(BF16)
    pl.semaphore_wait(barrier, len(met))

    def all_sum(it, gram):
        lines = deferred and it == 0
        return sum_everywhere(gram, lines, (parts_1, parts_2)[it], sum_send.at[it], sum_recv.at[it])

    def gathered(it):
        return gather((blocks_1, blocks_2)[it], gather_send, gather_recv.at[it])

    def images_of(it):
        refs = ((blocks_1, partial_1, arrived_1), (blocks_2, partial_2, arrived_2))[it]
        return images(columns, counts, tiles, *refs, image_send, image_recv.at[it])

    def keep(image):
        for b in range(BP):
            blocks_2[row * BP + b] = image[:, b * size : (b + 1) * size].astype(BF16)

    def tell_beside_x(turn):
        for to in beside_x:
            pl.semaphore_signal(known.at[turn], inc=1, device_id=to, device_id_type=MESH)

    pieces = gathered(0)
    advance(pieces, 6)
    tell_beside_x(0)
    advance(pieces, 7)
    pl.semaphore_wait(known.at[0], 2)
    tell_beside_x(1)
    advance(pieces, len(GATHER) + 1 - 13)
    load.wait()
    pl.semaphore_wait(known.at[1], 2)
    shares = images_of(0)
    next(shares)
    last(pieces)
    image = next(shares)

    if deferred:
        keep(image)
        pieces = gathered(1)
        next(pieces)
        last(shares)
        first_total = all_sum(0, gram_of(image))
        next(first_total)
        advance(pieces, len(GATHER))
        next(first_total)
        shares = images_of(1)
        next(shares)
        last(pieces)
        next(first_total)
        image = next(shares)
        total = all_sum(1, gram_of(image))
        advance(total, 2)
        next(first_total)
        last(shares)
        next(total)
        first_gram = next(first_total)
        last(first_total)
        _, first_inverse = factor(first_gram)
        first_growth, _, _ = growth(first_gram, first_inverse)
    else:
        last(shares)
        total = all_sum(0, gram_of(image))
        advance(total, 3)
        _, inverse = factor(next(total))
        last(total)
        keep(jnp.dot(inverse, image, precision=HIGHEST, preferred_element_type=F32))
        pieces = gathered(1)
        advance(pieces, len(GATHER) + 1)
        shares = images_of(1)
        next(shares)
        last(pieces)
        image = next(shares)
        last(shares)
        total = all_sum(1, gram_of(image))
        advance(total, 3)
    gram = next(total)

    upper, inverse = factor(gram)
    vectors = jnp.dot(inverse, image, precision=HIGHEST, preferred_element_type=F32)
    for b in range(BP):
        embedding[b] = vectors[:, b * size : (b + 1) * size] * scaling
    if deferred:
        upper = lax.dot_general(
            upper, first_inverse, (((1,), (1,)), ((), ())), precision=HIGHEST, preferred_element_type=F32
        )
        second_growth, least, most = growth(gram, inverse)
        safe = (first_growth < MAX_GROWTH) & (second_growth < MAX_GROWTH) & (least > 1e-18) & (most < 1e34)
        flag[0, 0] = safe.astype(jnp.int32)
    upper_out[...] = upper * (1.0 / scaling)
    last(total)


def call(deferred, affinity_tiles, columns, counts, start_vectors):
    rows = affinity_tiles.shape[0]
    pieces, vecs, size = start_vectors.shape
    scaling = math.sqrt(ROWS * COLS * BP * size)
    vmem, smem = pl.BlockSpec(memory_space=pltpu.VMEM), pl.BlockSpec(memory_space=pltpu.SMEM)
    hbm = pl.BlockSpec(memory_space=pl.ANY)
    dma = pltpu.SemaphoreType.DMA
    sent = [BF16 if deferred and narrow else F32 for narrow in NARROW]
    outs = [jax.ShapeDtypeStruct(start_vectors.shape, F32), jax.ShapeDtypeStruct((vecs, vecs), F32)]
    return pl.pallas_call(
        functools.partial(kernel, deferred, scaling),
        out_shape=outs + [jax.ShapeDtypeStruct((1, 1), jnp.int32)] * deferred,
        in_specs=[smem, smem, hbm, hbm],
        out_specs=[vmem, vmem] + [smem] * deferred,
        scratch_shapes=[pltpu.VMEM((ROWS * BP + 1, vecs, size), BF16)] * ITERS
        + [pltpu.VMEM((rows, vecs, size), dtype) for dtype in sent]
        + [pltpu.VMEM((COLS, pieces, vecs, size), dtype) for dtype in sent]
        + [
            pltpu.VMEM(start_vectors.shape, F32),
            pltpu.VMEM(affinity_tiles.shape, BF16),
            pltpu.VMEM((SUM_SLOTS, 3 * vecs // 8, 2 * vecs), F32),
            pltpu.VMEM((SUM_SLOTS, 3 * vecs // 8, 2 * vecs), F32),
            dma((2,)),
            dma((GATHER_SENDS,)),
            dma((ITERS, len(CHUNKS) * GATHER_SLOTS)),
            dma((COLS,)),
            dma((ITERS, COLS)),
            dma((ITERS, SUM_SLOTS)),
            dma((ITERS, SUM_SLOTS)),
            pltpu.SemaphoreType.REGULAR((2,)),
        ],
        compiler_params=pltpu.CompilerParams(
            collective_id=int(deferred), has_side_effects=True, vmem_limit_bytes=48 * 1024 * 1024
        ),
        name="deferred" if deferred else "in_order",
    )(columns, counts, start_vectors, affinity_tiles)


def body(affinity_tiles, block_columns, slot_counts, start_vectors):
    args = (affinity_tiles, block_columns.T, slot_counts.T, start_vectors)
    embedding, upper, safe = call(True, *args)
    return lax.cond(safe[0, 0] > 0, lambda: (embedding, upper), lambda: tuple(call(False, *args)))


def solution(mesh):
    in_specs = (
        P("row", "col", None, None),
        P("row", "col"),
        P("row", "col"),
        P(("row", "col"), None, None),
    )
    out_specs = (P(("row", "col"), None, None), P())
    return jax.shard_map(body, mesh=mesh, in_specs=in_specs, out_specs=out_specs, check_vma=False)
```

```python
import functools
import math

import jax
import jax.numpy as jnp
from jax import lax
from jax.experimental import pallas as pl
from jax.experimental.pallas import tpu as pltpu
from jax.sharding import PartitionSpec as P

ITERS = 2
MESH = pl.DeviceIdType.MESH
F32 = jnp.float32
BF16 = jnp.bfloat16
HIGHEST = lax.Precision.HIGHEST
X, Y, Z = 4, 4, 8
COLS = 8
SLOTS = 8
BP = 4
ROWS = 32
PIVOTS = 8
MAX_GROWTH = 1.15
NARROW = (True, True)

CHUNKS = ((0, 4),)
GATHER = (
    ((0, 0), 0, (("z", 2), ("z", -2), ("z", 1), ("z", -1), ("y", 0), ("s", 0))),
    ((0, 6), 0, (("y", 0), ("z", 2), ("z", 1), ("s", 0))),
    ((0, 2), 0, (("y", 0), ("z", -1), ("s", 0))),
    ((0, 7), 0, (("y", 0), ("s", 0))),
    ((0, 1), 0, (("y", 0), ("s", 0))),
    ((1, 0), 0, (("s", 0),)),
    ((1, 6), 0, (("z", 2), ("z", 1), ("s", 0))),
    ((1, 2), 0, (("z", -1), ("s", 0))),
    ((0, 5), 0, (("s", 0),)),
    ((0, 3), 0, (("s", 0),)),
    ((1, 7), 0, (("s", 0),)),
    ((1, 1), 0, (("s", 0),)),
    ((0, 4), 0, (("s", 0),)),
    ((1, 5), 0, (("s", 0),)),
    ((1, 3), 0, (("s", 0),)),
    ((1, 4), 0, (("s", 0),)),
)
GATHER_SENDS = sum(len(targets) for _, _, targets in GATHER)
GATHER_SLOTS = 4 * Z

SUM_SLOTS = 2 + X * Y + Z


def coords():
    row, col = lax.axis_index("row"), lax.axis_index("col")
    return lax.rem(col, 4), col // 4 * 2 + lax.rem(row // 2, 2), row // 4, lax.rem(row, 2)


def device(x, y, z, core):
    return (z * 4 + lax.rem(y, 2) * 2 + core, y // 2 * 4 + x)


def remote(src, dst, send_sem, recv_sem, to):
    return pltpu.make_async_remote_copy(
        src_ref=src, dst_ref=dst, send_sem=send_sem, recv_sem=recv_sem, device_id=to, device_id_type=MESH
    )


def gather(blocks, send_sem, recv_sem):
    x, y, z, core = coords()
    partner = y // 2 * 2 + 1 - lax.rem(y, 2)
    way = 1 - 2 * core

    def place(piece, chunk, core):
        column, dz = piece
        y_of = y if column == 0 else partner
        row = lax.rem(z + way * dz + Z, Z) * 4 + lax.rem(y_of, 2) * 2 + core
        return blocks.at[pl.ds(row * BP + CHUNKS[chunk][0], CHUNKS[chunk][1])]

    def slot(column, dz, chunk, other):
        return ((chunk * 2 + other) * 2 + column) * Z + dz

    def wait(piece, chunk, other):
        column, dz = piece
        here = place(piece, chunk, 1 - core if other else core)
        index = slot(column, -dz % Z if other else dz, chunk, other)
        remote(here, here, send_sem.at[0], recv_sem.at[index], device(x, y, z, 1 - core)).wait_recv()

    copies, held = [], [((0, 0), chunk) for chunk in range(len(CHUNKS))]
    for position, (piece, chunk, targets) in enumerate(GATHER):
        column, dz = piece
        if (piece, chunk) not in held:
            wait(piece, chunk, 0)
            held.append((piece, chunk))
        here = place(piece, chunk, core)
        for kind, step in targets:
            if kind == "z":
                to = device(x, y, lax.rem(z + way * step + Z, Z), core)
                index = slot(column, (dz - step) % Z, chunk, 0)
            elif kind == "y":
                to, index = device(x, partner, z, core), slot(1 - column, dz, chunk, 0)
            else:
                to, index = device(x, y, z, 1 - core), slot(column, dz, chunk, 1)
            copy = remote(here, here, send_sem.at[len(copies)], recv_sem.at[index], to)
            copy.start()
            copies.append(copy)
        yield position
    for piece, chunk in held:
        wait(piece, chunk, 1)
    yield
    for copy in copies:
        copy.wait_send()


def product(columns, counts, tiles, blocks, b):
    picked = []
    for s in range(SLOTS):
        name = columns[s, b]
        place = name // (COLS * BP) * BP + name % BP
        picked.append(blocks[jnp.where(s < counts[0, b], place, ROWS * BP)])
    vectors = jnp.concatenate(picked, axis=1)
    tile_row = jnp.concatenate([tiles[b, s] for s in range(SLOTS)], axis=1)
    return lax.dot_general(vectors, tile_row, (((1,), (1,)), ((), ())), preferred_element_type=F32)


def images(columns, counts, tiles, blocks, partial, arrived, send_sem, recv_sem):
    x, y, z, core = coords()
    col = lax.axis_index("col")

    def peer(offset):
        to_x, to_hi = lax.rem(x + offset, X), lax.rem(y // 2 + offset // X, 2)
        return to_hi * X + to_x, device(to_x, to_hi * 2 + lax.rem(y, 2), z, core)

    def copy(offset):
        owner, to = peer(offset)
        return remote(
            partial.at[pl.ds(owner * BP, BP)], arrived.at[offset], send_sem.at[offset], recv_sem.at[offset], to
        )

    def share(owner):
        return [product(columns, counts, tiles, blocks, owner * BP + within) for within in range(BP)]

    def send(offset):
        owner = peer(offset)[0]
        for within, image in enumerate(share(owner)):
            partial[owner * BP + within] = image.astype(partial.dtype)
        copy(offset).start()

    def step(i, carry):
        send(6 - i - 2 * (i // 2))
        send(7 - 3 * i + 2 * (i // 2))
        return carry

    lax.fori_loop(0, 3, step, 0)
    send(1)
    own = share(col)
    yield
    for offset in (6, 7, 5, 4, 2, 3, 1):
        copy(offset).wait_recv()
        for within in range(BP):
            own[within] = own[within] + arrived[offset, within].astype(F32)
    yield jnp.concatenate(own, axis=1)
    for offset in range(1, COLS):
        copy(offset).wait_send()


def stages(lines):
    x, y, z, core = coords()
    cores = (2, core, lambda o: device(x, y, z, 1 - core), lambda o: 1 - core, (1,))
    along_z = (
        Z,
        z,
        lambda o: device(x, y, lax.rem(z + o, Z), core),
        lambda o: lax.rem(z + o, Z),
        (4, 3, 5, 2, 6, 1, 7),
    )
    if lines:
        along_x = (X, x, lambda o: device(lax.rem(x + o, X), y, z, core), lambda o: lax.rem(x + o, X), (2, 1, 3))
        along_y = (Y, y, lambda o: device(x, lax.rem(y + o, Y), z, core), lambda o: lax.rem(y + o, Y), (2, 1, 3))
        return cores, along_x, along_y, along_z
    plane = (
        X * Y,
        y * X + x,
        lambda o: device(lax.rem(x + o, X), lax.rem(y + o // X, Y), z, core),
        lambda o: lax.rem(y + o // X, Y) * X + lax.rem(x + o, X),
        (10, 6, 9, 11, 14, 2, 5, 7, 8, 13, 15, 1, 3, 4, 12),
    )
    return cores, plane, along_z


def sum_everywhere(gram, lines, parts, send_sem, recv_sem):
    x, y, z, core = coords()
    half = gram.shape[0] // 2

    def fold(square):
        return jnp.concatenate([square[i : i + 8] for i in range(0, half, 8)], axis=1)

    def unfold(flat):
        return jnp.concatenate([flat[:, i : i + half] for i in range(0, 4 * half, half)], axis=0)

    total = jnp.concatenate([fold(gram[:half, :half]), fold(gram[:half, half:]), fold(gram[half:, half:])], axis=0)
    base, copies = 0, []
    for count, mine, to, source, order in stages(lines):
        sent, copies = copies, []
        here = parts.at[base + mine]
        here[...] = total
        for offset in order:
            copy = remote(here, here, send_sem.at[base + offset], recv_sem.at[base + mine], to(offset))
            copy.start()
            copies.append(copy)
        yield
        for copy in sent:
            copy.wait_send()
        for offset in order:
            there = parts.at[base + source(offset)]
            arrival = recv_sem.at[base + source(offset)]
            remote(there, there, send_sem.at[0], arrival, device(x, y, z, 1 - core)).wait_recv()
        total = parts[base]
        for i in range(1, count):
            total = total + parts[base + i]
        base += count
    first, cross, second = (unfold(total[i : i + 8]) for i in (0, 8, 16))
    yield jnp.concatenate(
        [jnp.concatenate([first, cross], axis=1), jnp.concatenate([cross.T, second], axis=1)], axis=0
    )
    for copy in copies:
        copy.wait_send()


def factor(gram):
    n = gram.shape[0]
    shape = (n, 2 * n)
    rows, cols = lax.broadcasted_iota(jnp.int32, shape, 0), lax.broadcasted_iota(jnp.int32, shape, 1)
    work = jnp.concatenate([gram, jnp.where(cols == rows, 1.0, 0.0).astype(F32)[:, :n]], axis=1)
    span = range(PIVOTS)
    for j in range(0, n, PIVOTS):
        rest, below = work[j:], rows[j:]
        top = [rest[p : p + 1] for p in span]
        entry = {(p, q): jnp.broadcast_to(top[p][:, j + q : j + q + 1], top[p].shape) for p in span for q in span if q >= p}
        column = [jnp.broadcast_to(rest[:, j + p : j + p + 1], rest.shape) for p in span]
        for p in span:
            inverse = 1.0 / entry[p, p]
            rest = rest - jnp.where(below > j + p, column[p], 0.0) * (top[p] * inverse)
            for q in range(p + 1, PIVOTS):
                ratio = entry[p, q] * inverse
                top[q] = top[q] - ratio * top[p]
                column[q] = column[q] - ratio * column[p]
                for r in range(q, PIVOTS):
                    entry[q, r] = entry[q, r] - ratio * entry[p, r]
        work = jnp.concatenate([work[:j], rest], axis=0) if j else rest
    pivots = jnp.sum(jnp.where(rows == cols, work, 0.0), axis=1, keepdims=True)
    work = work * lax.rsqrt(pivots)
    upper = jnp.where(rows <= cols, work, 0.0)[:, :n]
    return upper, work[:, n:]


def advance(steps, count):
    for _ in range(count):
        next(steps)


def last(steps):
    result = None
    for result in steps:
        pass
    return result


def gram_of(image):
    return lax.dot_general(image, image, (((1,), (1,)), ((), ())), precision=HIGHEST, preferred_element_type=F32)


def growth(gram, inverse):
    diagonal = lax.broadcasted_iota(jnp.int32, gram.shape, 0) == lax.broadcasted_iota(jnp.int32, gram.shape, 1)
    lengths = jnp.sum(jnp.where(diagonal, gram, 0.0), axis=0, keepdims=True)
    return jnp.sum(inverse * (inverse * lengths)) / gram.shape[0], jnp.min(lengths), jnp.max(lengths)


def kernel(deferred, scaling, columns, counts, start_in, tiles_in, embedding, upper_out, *rest):
    flag, rest = (rest[0], rest[1:]) if deferred else (None, rest)
    (blocks_1, blocks_2, partial_1, partial_2, arrived_1, arrived_2, start, tiles, parts_1, parts_2,
     load_sem, gather_send, gather_recv, image_send, image_recv, sum_send, sum_recv, known) = rest
    x, y, z, core = coords()
    barrier = pltpu.get_barrier_semaphore()
    beside_x = [device(lax.rem(x + o, X), y, z, core) for o in (1, X - 1)]
    met = [device(x, y, z, 1 - core)] + beside_x
    met += [device(x, lax.rem(y + o, Y), z, core) for o in (1, Y - 1)]
    met += [device(x, y, lax.rem(z + o, Z), core) for o in (1, 2, Z - 2, Z - 1)]
    load_start = pltpu.make_async_copy(start_in, start, load_sem.at[0])
    load_start.start()
    for to in met:
        pl.semaphore_signal(barrier, inc=1, device_id=to, device_id_type=MESH)
    load = pltpu.make_async_copy(tiles_in, tiles, load_sem.at[1])
    load.start()

    vecs, size = start.shape[1:]
    row = lax.axis_index("row")
    for ref in (blocks_1, blocks_2):
        ref[ROWS * BP] = jnp.zeros((vecs, size), BF16)
    load_start.wait()
    blocks_1[pl.ds(row * BP, BP)] = start[...].astype(BF16)
    pl.semaphore_wait(barrier, len(met))

    def all_sum(it, gram):
        lines = deferred and it == 0
        return sum_everywhere(gram, lines, (parts_1, parts_2)[it], sum_send.at[it], sum_recv.at[it])

    def gathered(it):
        return gather((blocks_1, blocks_2)[it], gather_send, gather_recv.at[it])

    def images_of(it):
        refs = ((blocks_1, partial_1, arrived_1), (blocks_2, partial_2, arrived_2))[it]
        return images(columns, counts, tiles, *refs, image_send, image_recv.at[it])

    def keep(image):
        for b in range(BP):
            blocks_2[row * BP + b] = image[:, b * size : (b + 1) * size].astype(BF16)

    def tell_beside_x(turn):
        for to in beside_x:
            pl.semaphore_signal(known.at[turn], inc=1, device_id=to, device_id_type=MESH)

    pieces = gathered(0)
    advance(pieces, 6)
    tell_beside_x(0)
    advance(pieces, 7)
    pl.semaphore_wait(known.at[0], 2)
    tell_beside_x(1)
    advance(pieces, len(GATHER) + 1 - 13)
    load.wait()
    pl.semaphore_wait(known.at[1], 2)
    shares = images_of(0)
    next(shares)
    last(pieces)
    image = next(shares)

    if deferred:
        keep(image)
        pieces = gathered(1)
        next(pieces)
        last(shares)
        first_total = all_sum(0, gram_of(image))
        next(first_total)
        advance(pieces, len(GATHER))
        next(first_total)
        shares = images_of(1)
        next(shares)
        last(pieces)
        next(first_total)
        image = next(shares)
        total = all_sum(1, gram_of(image))
        advance(total, 2)
        next(first_total)
        last(shares)
        next(total)
        first_gram = next(first_total)
        last(first_total)
        _, first_inverse = factor(first_gram)
        first_growth, _, _ = growth(first_gram, first_inverse)
    else:
        last(shares)
        total = all_sum(0, gram_of(image))
        advance(total, 3)
        _, inverse = factor(next(total))
        last(total)
        keep(jnp.dot(inverse, image, precision=HIGHEST, preferred_element_type=F32))
        pieces = gathered(1)
        advance(pieces, len(GATHER) + 1)
        shares = images_of(1)
        next(shares)
        last(pieces)
        image = next(shares)
        last(shares)
        total = all_sum(1, gram_of(image))
        advance(total, 3)
    gram = next(total)

    upper, inverse = factor(gram)
    vectors = jnp.dot(inverse, image, precision=HIGHEST, preferred_element_type=F32)
    for b in range(BP):
        embedding[b] = vectors[:, b * size : (b + 1) * size] * scaling
    if deferred:
        upper = lax.dot_general(
            upper, first_inverse, (((1,), (1,)), ((), ())), precision=HIGHEST, preferred_element_type=F32
        )
        second_growth, least, most = growth(gram, inverse)
        safe = (first_growth < MAX_GROWTH) & (second_growth < MAX_GROWTH) & (least > 1e-18) & (most < 1e34)
        flag[0, 0] = safe.astype(jnp.int32)
    upper_out[...] = upper * (1.0 / scaling)
    last(total)


def call(deferred, affinity_tiles, columns, counts, start_vectors):
    rows = affinity_tiles.shape[0]
    pieces, vecs, size = start_vectors.shape
    scaling = math.sqrt(ROWS * COLS * BP * size)
    vmem, smem = pl.BlockSpec(memory_space=pltpu.VMEM), pl.BlockSpec(memory_space=pltpu.SMEM)
    hbm = pl.BlockSpec(memory_space=pl.ANY)
    dma = pltpu.SemaphoreType.DMA
    sent = [BF16 if deferred and narrow else F32 for narrow in NARROW]
    outs = [jax.ShapeDtypeStruct(start_vectors.shape, F32), jax.ShapeDtypeStruct((vecs, vecs), F32)]
    return pl.pallas_call(
        functools.partial(kernel, deferred, scaling),
        out_shape=outs + [jax.ShapeDtypeStruct((1, 1), jnp.int32)] * deferred,
        in_specs=[smem, smem, hbm, hbm],
        out_specs=[vmem, vmem] + [smem] * deferred,
        scratch_shapes=[pltpu.VMEM((ROWS * BP + 1, vecs, size), BF16)] * ITERS
        + [pltpu.VMEM((rows, vecs, size), dtype) for dtype in sent]
        + [pltpu.VMEM((COLS, pieces, vecs, size), dtype) for dtype in sent]
        + [
            pltpu.VMEM(start_vectors.shape, F32),
            pltpu.VMEM(affinity_tiles.shape, BF16),
            pltpu.VMEM((SUM_SLOTS, 3 * vecs // 8, 2 * vecs), F32),
            pltpu.VMEM((SUM_SLOTS, 3 * vecs // 8, 2 * vecs), F32),
            dma((2,)),
            dma((GATHER_SENDS,)),
            dma((ITERS, len(CHUNKS) * GATHER_SLOTS)),
            dma((COLS,)),
            dma((ITERS, COLS)),
            dma((ITERS, SUM_SLOTS)),
            dma((ITERS, SUM_SLOTS)),
            pltpu.SemaphoreType.REGULAR((2,)),
        ],
        compiler_params=pltpu.CompilerParams(
            collective_id=int(deferred), has_side_effects=True, vmem_limit_bytes=48 * 1024 * 1024
        ),
        name="deferred" if deferred else "in_order",
    )(columns, counts, start_vectors, affinity_tiles)


def body(affinity_tiles, block_columns, slot_counts, start_vectors):
    args = (affinity_tiles, block_columns.T, slot_counts.T, start_vectors)
    embedding, upper, safe = call(True, *args)
    return lax.cond(safe[0, 0] > 0, lambda: (embedding, upper), lambda: tuple(call(False, *args)))


def solution(mesh):
    in_specs = (
        P("row", "col", None, None),
        P("row", "col"),
        P("row", "col"),
        P(("row", "col"), None, None),
    )
    out_specs = (P(("row", "col"), None, None), P())
    return jax.shard_map(body, mesh=mesh, in_specs=in_specs, out_specs=out_specs, check_vma=False)
```
